32 devices in a mesh: prow: 8 (over z, y), pcol: 4 (over x, core).
Axes of the slice: x: 2, y: 2, z: 4, core: 2. Of those that a mesh axis runs over, the one named last changes fastest.
Arguments:
- anc_inverse: float32 [2048, 2048], P('prow', 'pcol'), as said below
- factor_one: float32 [2048, 2048], P('prow', 'pcol'), may hold values from -0.1875 to 0.1875
- pivot_one: float32 [8, 256, 256], P('pcol')
- factor_two: float32 [2048, 2048], P('prow', 'pcol'), may hold values from -0.25 to 0.25
- factor_link: float32 [16, 256, 128], P('pcol'), may hold values from -0.375 to 0.375
- pivot_two: float32 [16, 128, 128], P('pcol')
- pattern_one: int32 [8, 8], replicated, may hold values 0 or 1
- pattern_two: int32 [8, 16], replicated, may hold values 0 or 1
- parent_two: int32 [16], replicated, may hold values from 0 to 7, as said below
- size_one: int32 [8], replicated, may hold values from 64 to 256
- size_two: int32 [16], replicated, may hold values from 64 to 128
Outputs:
- inverse_one: float32 [2048, 2048], P('prow', 'pcol')
- diagonal_one: float32 [8, 256, 256], P('pcol')
- inverse_two: float32 [2048, 2048], P('prow', 'pcol')
- inverse_link: float32 [16, 256, 128], P('pcol')
- diagonal_two: float32 [16, 128, 128], P('pcol')
The draws below stay inside these ranges and needn't reach their ends.
Inputs may be any that keep to these rules, and one draw needn't show every extreme that they name: anc_inverse is exactly symmetric. `parent_two`: the parent of a level-2 supernode K in [c * 4, (c + 1) * 4) lies in [c * 2, (c + 1) * 2); every level-1 supernode has exactly two children.
All inputs are finite; a program needn't handle non-finite values.
Results may differ from the reference program's by a relative error of at most 0.000078.
Values sent between devices are 32-bit elements; how exact they have to be, the bound alone decides.
No kernel may reach another device: no remote copies, remote signals or barrier semaphores. Data moves between devices by JAX's collectives and lax.ppermute only.
A program may use at most 128 MiB of HBM per device.

```python
import jax
import jax.numpy as jnp
from jax import lax

B1 = 256
B2 = 128
J1_COL = 2
J2_COL = 4
NA = 8
NJ1 = 8
NK = 16


def symmetric_blocks(base, width, strength):
    scaled = base * width ** (-0.5)
    paired = (scaled + jnp.swapaxes(scaled, 1, 2)) * 0.7071
    return jnp.eye(width, dtype=jnp.float32)[None, :, :] + strength * paired


def ragged_sizes(key, count, width, lowest):
    values = jax.random.randint(key, (count,), lowest, width + 1)
    target = jax.random.randint(jax.random.fold_in(key, 1), (), 0, count)
    return jnp.where(jnp.arange(count) == target, width, values).astype(jnp.int32)


def draw_anc_inverse(key, part):
    key = jax.random.fold_in(key, 11)
    total = NA * B1
    base = jax.random.normal(key, (1, total, total), jnp.float32)
    return symmetric_blocks(base, total, 0.4)[0]


def draw_pivot_one(key, part):
    key = jax.random.fold_in(key, 12)
    base = jax.random.normal(key, (NJ1, B1, B1), jnp.float32)
    return symmetric_blocks(base, B1, 0.3)


def draw_pivot_two(key, part):
    key = jax.random.fold_in(key, 13)
    base = jax.random.normal(key, (NK, B2, B2), jnp.float32)
    return symmetric_blocks(base, B2, 0.3)


def draw_parent_two(key, part):
    key = jax.random.fold_in(key, 14)
    columns = NK // J2_COL
    keys = jax.random.split(key, columns)
    local = jax.vmap(lambda k: jax.random.permutation(k, J2_COL))(keys) // 2
    offsets = (jnp.arange(columns) * J1_COL)[:, None]
    return (local + offsets).reshape(NK).astype(jnp.int32)


def draw_size_one(key, part):
    key = jax.random.fold_in(key, 15)
    return ragged_sizes(key, NJ1, B1, B1 // 4)


def draw_size_two(key, part):
    key = jax.random.fold_in(key, 16)
    return ragged_sizes(key, NK, B2, B2 // 2)


def with_ends(drawn, own_key, smallest, top_value):
    extent = drawn.shape
    place = [jax.random.randint(jax.random.fold_in(own_key, axis), (), 0, extent[axis]) for axis in range(len(extent))]
    drawn = drawn.at[tuple(place)].set(smallest)
    longest = extent.index(max(extent))
    place[longest] = (place[longest] + 1) % extent[longest]
    return drawn.at[tuple(place)].set(top_value)


def steps_of(key, dims, cuts, low, top_value):
    factor_of = 1.0
    for position, parts in cuts:
        steps = jax.random.uniform(jax.random.fold_in(jax.random.fold_in(key, 6), position), (parts,), jnp.float32, low / len(cuts), top_value / len(cuts))
        factor_of = factor_of * jnp.repeat(jnp.exp(steps), dims[position] // parts).reshape((-1,) + (1,) * (len(dims) - 1 - position))
    return factor_of


def centred(own_key, shape, spread, reach, cuts=(), held_as=jnp.bfloat16):
    loudness = steps_of(own_key, shape, cuts, -0.22, 0.18) if cuts else 1.0
    entries = jax.random.normal(own_key, shape, jnp.float32) * spread * loudness
    return jnp.minimum(jnp.maximum(entries, -reach), reach).astype(held_as)


def setup_inputs(seed: int = 0) -> dict:
    streams_of = jax.random.split(jax.random.key(seed), 12)
    return {
        "anc_inverse": draw_anc_inverse(jax.random.fold_in(streams_of[11], 71), 0),
        "factor_one": centred(streams_of[1], (NA * B1, NJ1 * B1), (NA * B1 // 2) ** -0.5, 0.1875, ((0, 8), (1, 4)), jnp.float32),
        "pivot_one": draw_pivot_one(jax.random.fold_in(streams_of[11], 71), 0),
        "factor_two": centred(streams_of[3], (NA * B1, NK * B2), (NA * B1 // 4) ** -0.5, 0.25, ((0, 8), (1, 4)), jnp.float32),
        "factor_link": centred(streams_of[4], (NK, B1, B2), B1 ** -0.5, 0.375, ((0, 4),), jnp.float32),
        "pivot_two": draw_pivot_two(jax.random.fold_in(streams_of[11], 71), 0),
        "pattern_one": with_ends((jax.random.randint(streams_of[6], (NA, NJ1), 0, 2) < 1).astype(jnp.int32), jax.random.fold_in(streams_of[6], 1), 0, 1),
        "pattern_two": with_ends((jax.random.randint(streams_of[7], (NA, NK), 0, 2) < 1).astype(jnp.int32), jax.random.fold_in(streams_of[7], 1), 0, 1),
        "parent_two": draw_parent_two(jax.random.fold_in(streams_of[11], 71), 0),
        "size_one": draw_size_one(jax.random.fold_in(streams_of[11], 71), 0),
        "size_two": draw_size_two(jax.random.fold_in(streams_of[11], 71), 0),
    }


PRECISE = lax.Precision.HIGHEST


def block_repeat(blocks, height, width):
    return jnp.repeat(jnp.repeat(blocks, height, axis=0), width, axis=1)


def size_mask(sizes, width):
    return (jnp.arange(width)[None, :] < sizes[:, None]).astype(jnp.float32)


def reference(anc_inverse, factor_one, pivot_one, factor_two, factor_link, pivot_two, pattern_one, pattern_two, parent_two, size_one, size_two):
    cols_one = size_mask(size_one, B1)
    cols_two = size_mask(size_two, B2)
    first_pattern = pattern_one.astype(jnp.float32)
    blocks_one = block_repeat(first_pattern, B1, B1)
    low_one = factor_one * blocks_one * cols_one.reshape(1, -1)
    inverse_one = -jnp.dot(anc_inverse, low_one, precision=PRECISE) * blocks_one
    low_three = low_one.reshape(NA * B1, NJ1, B1)
    inverse_three = inverse_one.reshape(NA * B1, NJ1, B1)
    pivots_one = pivot_one * cols_one[:, :, None] * cols_one[:, None, :]
    diagonal_one = pivots_one - jnp.einsum("ija,ijb->jab", low_three, inverse_three, precision=PRECISE)
    mask_two = pattern_two.astype(jnp.float32) * first_pattern[:, parent_two]
    blocks_two = block_repeat(mask_two, B1, B2)
    low_two = factor_two * blocks_two * cols_two.reshape(1, -1)
    link = factor_link * cols_one[parent_two][:, :, None] * cols_two[:, None, :]
    parent_cols = inverse_three[:, parent_two, :]
    near = jnp.einsum("ikb,kbd->ikd", parent_cols, link, precision=PRECISE).reshape(NA * B1, NK * B2)
    inverse_two = -(near + jnp.dot(anc_inverse, low_two, precision=PRECISE)) * blocks_two
    second_three = low_two.reshape(NA * B1, NK, B2)
    inverse_four = inverse_two.reshape(NA * B1, NK, B2)
    inverse_link = -(jnp.einsum("kab,kbd->kad", diagonal_one[parent_two], link, precision=PRECISE)
                     + jnp.einsum("ika,ikd->kad", parent_cols, second_three, precision=PRECISE))
    pivots_two = pivot_two * cols_two[:, :, None] * cols_two[:, None, :]
    diagonal_two = (pivots_two - jnp.einsum("kbd,kbe->kde", link, inverse_link, precision=PRECISE)
                    - jnp.einsum("ikd,ike->kde", second_three, inverse_four, precision=PRECISE))
    return inverse_one, diagonal_one, inverse_two, inverse_link, diagonal_two
```

```python
import jax
import jax.numpy as jnp
from jax import lax
from jax.sharding import PartitionSpec as P

PRECISE = lax.Precision.HIGH
AXES = ("prow", "pcol")
CHUNKS = 1


def matmul(left, right, dims):
    return lax.dot_general(left, right, (dims, ((), ())), precision=PRECISE)


def size_mask(size, width):
    return (jnp.arange(width) < size).astype(jnp.float32)


def solution(mesh):
    rows_of, cols_of = mesh.shape["prow"], mesh.shape["pcol"]
    depth, wide = rows_of // 2, cols_of // 2

    def pairs(move):
        out = []
        for z in range(depth):
            for y in range(2):
                for x in range(wide):
                    for k in range(2):
                        to = move(z, y, x, k)
                        if to is not None:
                            a, b, c, d = to
                            out.append(
                                ((z * 2 + y) * cols_of + x * 2 + k, (a * 2 + b) * cols_of + c * 2 + d)
                            )
        return out

    to_worker = pairs(lambda z, y, x, k: (z, y, x, 1 - k) if k == y else (z, 1 - y, x, k))
    to_home = pairs(lambda z, y, x, k: (z, 1 - y, x, k) if k == y else (z, y, x, 1 - k))
    across = pairs(lambda z, y, x, k: None if k == y else (z, 1 - y, x, 1 - k))
    other_y = pairs(lambda z, y, x, k: (z, 1 - y, x, k))
    other_core = pairs(lambda z, y, x, k: (z, y, x, 1 - k))
    up = pairs(lambda z, y, x, k: (z + 1, y, x, k) if z + 1 < depth else None)
    down = pairs(lambda z, y, x, k: (z - 1, y, x, k) if z > 0 else None)

    def send(value, perm):
        return lax.ppermute(value, AXES, perm)

    def on_device(
        anc_inverse,
        factor_one,
        pivot_one,
        factor_two,
        factor_link,
        pivot_two,
        pattern_one,
        pattern_two,
        parent_two,
        size_one,
        size_two,
    ):
        rows, tile = anc_inverse.shape
        b1, b2 = pivot_one.shape[1], pivot_two.shape[1]
        my_row, my_col = lax.axis_index("prow"), lax.axis_index("pcol")
        z, y = my_row // 2, my_row % 2
        x, k = my_col // 2, my_col % 2
        stays = k == y
        base_one, base_two = my_col * 2, my_col * 4
        parents = [parent_two[base_two + i] - base_one for i in range(4)]
        place = [
            2 * parents[i] + sum([(parents[j] == parents[i]).astype(jnp.int32) for j in range(i)], 0)
            for i in range(4)
        ]
        order = [
            sum([jnp.where(place[i] == j, i, 0) for i in range(1, 4)], 0).astype(jnp.int32) for j in range(4)
        ]
        on_one = [pattern_one[my_row, base_one + f].astype(jnp.float32) for f in range(2)]
        on_two = [
            pattern_two[my_row, base_two + order[j]].astype(jnp.float32) * on_one[j // 2] for j in range(4)
        ]
        live_one = [size_mask(size_one[base_one + f], b1) for f in range(2)]
        live_two = [size_mask(size_two[base_two + order[j]], b2) for j in range(4)]
        first = [factor_one[:, f * b1 : (f + 1) * b1] * (on_one[f] * live_one[f])[None, :] for f in range(2)]
        second = [
            jnp.concatenate(
                [
                    lax.dynamic_slice_in_dim(factor_two, order[j] * b2, b2, 1) * (on_two[j] * live_two[j])[None, :]
                    for j in (2 * f, 2 * f + 1)
                ],
                axis=1,
            )
            for f in range(2)
        ]

        def fetch(mine):
            kept = jnp.where(y == 0, mine[0], mine[1])
            near = send(jnp.where(y == 0, mine[1], mine[0]), to_worker)
            far = send(kept, across)
            same = jnp.where(stays, kept, near)
            other = jnp.where(stays, near, far)
            return jnp.concatenate([jnp.where(y == 0, same, other), jnp.where(y == 0, other, same)], axis=0)

        w1 = fetch(first)
        beside = send(anc_inverse, other_y)

        def stacked(own, received):
            return jnp.concatenate(
                [jnp.where(y == 0, own, received), jnp.where(y == 0, received, own)], axis=0
            )

        tiles = [(x, stacked(anc_inverse, beside))]
        for s in range(1, wide):
            turn = pairs(lambda z, y, x, k: (z, y, (x + s) % wide, k))
            tiles.append(((x + wide - s) % wide, stacked(send(anc_inverse, turn), send(beside, turn))))
        panel = jnp.zeros((2 * rows, tile * cols_of), jnp.float32)
        for at, value in tiles:
            panel = lax.dynamic_update_slice(panel, value, (0, (at * 2 + k) * tile))
        for at, value in tiles:
            panel = lax.dynamic_update_slice(panel, send(value, other_core), (0, (at * 2 + 1 - k) * tile))
        w2 = fetch(second)
        span = 2 * rows
        parts = matmul(panel, w2, ((0,), (0,)))

        def part(d):
            d = jnp.clip(d, 0, depth - 1)
            return lax.dynamic_slice_in_dim(parts, d * span, span, 0)

        held = jnp.zeros(((3 * depth - 2) * span, b1), jnp.float32)
        held = lax.dynamic_update_slice(held, w1, ((z + depth - 1) * span, 0))
        from_below = from_above = w1
        for s in range(1, depth + 1):
            go_up, go_down = from_below, from_above
            if s > 1:
                go_up = go_up + jnp.where(z <= s - 2, part(z + 1 + depth - s), 0.0)
                back = depth - 1 - z
                go_down = go_down + jnp.where(back <= s - 2, part(z - 1 - depth + s), 0.0)
            from_below, from_above = send(go_up, up), send(go_down, down)
            if s < depth:
                held = lax.dynamic_update_slice(held, from_below, ((z - s + depth - 1) * span, 0))
                held = lax.dynamic_update_slice(held, from_above, ((z + s + depth - 1) * span, 0))
        whole = held[(depth - 1) * span : (2 * depth - 1) * span]
        y1 = matmul(panel, whole, ((1,), (0,)))
        y2 = part(z) + from_below + from_above
        grams = jnp.concatenate([matmul(w1, y1, ((0,), (0,))), matmul(y1, w2, ((0,), (0,)))], axis=1)
        energy = jnp.concatenate(
            [matmul(w2[:, j * b2 : (j + 1) * b2], y2[:, j * b2 : (j + 1) * b2], ((0,), (0,))) for j in range(2)],
            axis=1,
        )

        def total(value):
            step = 1
            while step < depth:
                value = value + send(value, pairs(lambda z, y, x, k: (z ^ step, y, x, k)))
                step *= 2
            return value

        def deliver(same, other):
            near = send(jnp.where(stays, other, same), to_home)
            far = send(other, across)
            mine = jnp.where(stays, same, far)
            return [jnp.where(y == 0, mine, near), jnp.where(y == 0, near, mine)]

        def split(value):
            lower, upper = value[:rows], value[rows:]
            return jnp.where(y == 0, lower, upper), jnp.where(y == 0, upper, lower)

        home_one = deliver(*split(y1))
        home_two = deliver(*split(y2))
        grams = total(grams)
        grams = deliver(grams, grams)
        energy = total(energy)
        energy = deliver(energy, energy)
        out_one, out_diag, out_two, out_link, out_last = [], [], [None] * 4, [None] * 4, [None] * 4
        for f in range(2):
            out_one.append(-home_one[f] * on_one[f])
            diag = pivot_one[f] * live_one[f][:, None] * live_one[f][None, :] + grams[f][:, :b1]
            out_diag.append(diag)
            for j in (2 * f, 2 * f + 1):
                cut = slice((j - 2 * f) * b2, (j - 2 * f + 1) * b2)
                link = (
                    lax.dynamic_index_in_dim(factor_link, order[j], 0, keepdims=False)
                    * live_one[f][:, None]
                    * live_two[j][None, :]
                )
                near = matmul(home_one[f], link, ((1,), (0,)))
                out_two[j] = on_two[j] * (near - home_two[f][:, cut])
                cross = grams[f][:, b1:][:, cut]
                down_link = cross - matmul(diag, link, ((1,), (0,)))
                out_link[j] = down_link
                pivot = (
                    lax.dynamic_index_in_dim(pivot_two, order[j], 0, keepdims=False)
                    * live_two[j][:, None]
                    * live_two[j][None, :]
                )
                out_last[j] = (
                    pivot
                    - matmul(link, down_link, ((0,), (0,)))
                    - matmul(cross, link, ((0,), (0,)))
                    + energy[f][:, cut]
                )

        def unsorted(values):
            stack = jnp.stack(values)
            return [lax.dynamic_index_in_dim(stack, place[i], 0, keepdims=False) for i in range(4)]

        return (
            jnp.concatenate(out_one, axis=1),
            jnp.stack(out_diag),
            jnp.concatenate(unsorted(out_two), axis=1),
            jnp.stack(unsorted(out_link)),
            jnp.stack(unsorted(out_last)),
        )

    return jax.shard_map(
        on_device,
        mesh=mesh,
        in_specs=(
            P("prow", "pcol"),
            P("prow", "pcol"),
            P("pcol", None, None),
            P("prow", "pcol"),
            P("pcol", None, None),
            P("pcol", None, None),
            P(),
            P(),
            P(),
            P(),
            P(),
        ),
        out_specs=(
            P("prow", "pcol"),
            P("pcol", None, None),
            P("prow", "pcol"),
            P("pcol", None, None),
            P("pcol", None, None),
        ),
        check_vma=False,
    )
```

```python
import functools

import jax
import jax.numpy as jnp
from jax import lax
from jax.experimental import pallas as pl
from jax.experimental.pallas import tpu as pltpu
from jax.sharding import PartitionSpec as P

AXES = ("prow", "pcol")
F32 = jnp.float32
VMEM = pl.BlockSpec(memory_space=pltpu.VMEM)
SMEM = pl.BlockSpec(memory_space=pltpu.SMEM)
NN = ((1,), (0,))
NT = ((1,), (1,))
TN = ((0,), (0,))


def halves(value):
    high = value.astype(jnp.bfloat16)
    return high, (value - high.astype(F32)).astype(jnp.bfloat16)


def dot3(left, right, dims):
    def one(a, b):
        return lax.dot_general(a, b, (dims, ((), ())), preferred_element_type=F32)

    return one(left[0], right[0]) + (one(left[0], right[1]) + one(left[1], right[0]))


def place_of():
    my_row, my_col = lax.axis_index("prow"), lax.axis_index("pcol")
    return my_row // 2, my_row % 2, my_col // 2, my_col % 2


def family_order(parent_ref, my_col):
    parents = [parent_ref[my_col * 4 + i] - my_col * 2 for i in range(4)]
    place = []
    for i in range(4):
        seen = jnp.int32(0)
        for j in range(i):
            seen += jnp.where(parents[j] == parents[i], 1, 0)
        place.append(2 * parents[i] + seen)
    order = []
    for j in range(4):
        found = jnp.int32(0)
        for i in range(1, 4):
            found += jnp.where(place[i] == j, i, 0)
        order.append(found)
    return order


def below(size, shape, axis):
    return (lax.broadcasted_iota(jnp.int32, shape, axis) < size).astype(F32)


def pick(values, index):
    out = values[0]
    for i in range(1, len(values)):
        out = jnp.where(index == i, values[i], out)
    return out


def pack_one(block, factor_ref, pattern_ref, size_ref, kept_ref, give_ref):
    my_row, my_col = lax.axis_index("prow"), lax.axis_index("pcol")
    y = my_row % 2
    for out_ref, f in ((kept_ref, y), (give_ref, 1 - y)):
        values = factor_ref[:, pl.ds(pl.multiple_of(f * block, 128), block)]
        on = pattern_ref[my_row, my_col * 2 + f].astype(F32)
        keep = below(size_ref[my_col * 2 + f], values.shape, 1) * on
        out_ref[...] = (values * keep).T


def pack_two(
    block, factor_ref, first_ref, second_ref, parent_ref, size_ref, kept_ref, give_ref
):
    my_row, my_col = lax.axis_index("prow"), lax.axis_index("pcol")
    y = my_row % 2
    order = family_order(parent_ref, my_col)
    for out_ref, f in ((kept_ref, y), (give_ref, 1 - y)):
        for i in range(2):
            child = pick([order[i], order[2 + i]], f)
            values = factor_ref[:, pl.ds(pl.multiple_of(child * block, 128), block)]
            on = first_ref[my_row, my_col * 2 + f] * second_ref[my_row, my_col * 4 + child]
            keep = below(size_ref[my_col * 4 + child], values.shape, 1) * on.astype(F32)
            out_ref[i * block : (i + 1) * block, :] = (values * keep).T


def join(kept_ref, near_ref, far_ref, out_ref):
    _, y, _, k = place_of()
    rows = kept_ref.shape[1]

    @pl.when(k == y)
    def _():
        out_ref[:, :rows] = kept_ref[...]
        out_ref[:, rows:] = near_ref[...]

    @pl.when(k != y)
    def _():
        out_ref[:, :rows] = near_ref[...]
        out_ref[:, rows:] = far_ref[...]


def partial_products(wide, w2_ref, *refs):
    tiles, (parts_ref, high_ref, low_ref) = refs[:-3], refs[-3:]
    _, y, x, k = place_of()
    rows, tile = tiles[0].shape
    w2 = halves(w2_ref[...])
    same = (w2[0][:, :rows], w2[1][:, :rows])
    other = (w2[0][:, rows:], w2[1][:, rows:])
    for s in range(wide):
        for c in range(2):
            top, bottom = tiles[(s * 2 + c) * 2], tiles[(s * 2 + c) * 2 + 1]
            first = (lax.rem(x + wide - s, wide) * 2 + (k if c == 0 else 1 - k)) * (tile // rows)
            for b in range(tile // rows):
                block = first + b
                block = block - lax.rem(block, 2) + jnp.where(y == 0, lax.rem(block, 2), 1 - lax.rem(block, 2))
                at = pl.ds(pl.multiple_of(block * rows, 128), rows)
                cut = slice(b * rows, (b + 1) * rows)
                a = halves(top[:, cut])
                high_ref[:rows, at], low_ref[:rows, at] = a
                done = dot3(same, a, NN)
                a = halves(bottom[:, cut])
                high_ref[rows:, at], low_ref[rows:, at] = a
                parts_ref[:, at] = done + dot3(other, a, NN)


def combine(depth, s, up_ref, down_ref, part_up_ref, part_down_ref, go_up_ref, go_down_ref):
    z = lax.axis_index("prow") // 2

    @pl.when(z <= s - 2)
    def _():
        go_up_ref[...] = up_ref[...] + part_up_ref[...]

    @pl.when(z > s - 2)
    def _():
        go_up_ref[...] = up_ref[...]

    @pl.when(depth - 1 - z <= s - 2)
    def _():
        go_down_ref[...] = down_ref[...] + part_down_ref[...]

    @pl.when(depth - 1 - z > s - 2)
    def _():
        go_down_ref[...] = down_ref[...]


def gram_products(depth, high_ref, low_ref, w1_ref, w2_ref, *refs):
    taken = refs[: 2 * (depth - 1)]
    same_ref, other_ref, give_ref, mine_ref, theirs_ref, total_ref = refs[2 * (depth - 1) :]
    z, y, _, k = place_of()
    span = w1_ref.shape[1]
    rows = span // 2

    def product(ref, at):
        columns = pl.ds(pl.multiple_of(at * span, 128), span)
        return dot3(halves(ref[...]), (high_ref[:, columns], low_ref[:, columns]), NT)

    total_ref[...] = product(w1_ref, z)
    for s in range(1, depth):

        @pl.when(z >= s)
        def _():
            total_ref[...] += product(taken[2 * s - 2], z - s)

        @pl.when(z + s < depth)
        def _():
            total_ref[...] += product(taken[2 * s - 1], z + s)

    same_ref[...] = total_ref[:, :rows]
    other_ref[...] = total_ref[:, rows:]
    give_ref[...] = jnp.where(k == y, total_ref[:, rows:], total_ref[:, :rows])
    y1 = halves(total_ref[...])
    w1, w2 = halves(w1_ref[...]), halves(w2_ref[...])
    half, wide = mine_ref.shape[0], w1_ref.shape[0]
    for out_ref, start in ((mine_ref, z % 2), (theirs_ref, 1 - z % 2)):
        cut = pl.ds(pl.multiple_of(start * half, 8), half)
        out_ref[:, :wide] = dot3(halves(w1_ref[cut, :]), y1, NT)
        out_ref[:, wide:] = dot3(halves(total_ref[cut, :]), w2, NT)


def energy_products(part_ref, up_ref, down_ref, w2_ref, same_ref, other_ref, give_ref, energy_ref):
    _, y, _, k = place_of()
    rows = same_ref.shape[1]
    y2 = part_ref[...] + up_ref[...] + down_ref[...]
    same_ref[...] = y2[:, :rows]
    other_ref[...] = y2[:, rows:]
    give_ref[...] = jnp.where(k == y, y2[:, rows:], y2[:, :rows])
    y2, w2 = halves(y2), halves(w2_ref[...])
    block = energy_ref.shape[0]
    for i in range(2):
        cut = slice(i * block, (i + 1) * block)
        energy_ref[:, cut] = dot3((w2[0][cut], w2[1][cut]), (y2[0][cut], y2[1][cut]), NT)


def finish_rows(
    own1, near1, far1, own2, near2, far2, link_ref, first_ref, second_ref, parent_ref, one_ref, two_ref, out1, out2
):
    my_row, my_col = lax.axis_index("prow"), lax.axis_index("pcol")
    y, k = my_row % 2, my_col % 2
    b1, b2 = link_ref.shape[1:]
    order = family_order(parent_ref, my_col)
    for f, y1, y2 in (
        (1 - y, near1[...], near2[...]),
        (y, jnp.where(k == y, own1[...], far1[...]), jnp.where(k == y, own2[...], far2[...])),
    ):
        y1, y2 = y1.T, y2.T
        on = first_ref[my_row, my_col * 2 + f]
        out1[:, pl.ds(pl.multiple_of(f * b1, 128), b1)] = -y1 * on.astype(F32)
        y1 = halves(y1)
        for i in range(2):
            child = pick([order[i], order[2 + i]], f)
            link = (
                link_ref[child]
                * below(one_ref[my_col * 2 + f], (b1, b2), 0)
                * below(two_ref[my_col * 4 + child], (b1, b2), 1)
            )
            both = (on * second_ref[my_row, my_col * 4 + child]).astype(F32)
            near = dot3(y1, halves(link), NN)
            out2[:, pl.ds(pl.multiple_of(child * b2, 128), b2)] = (near - y2[:, i * b2 : (i + 1) * b2]) * both


def finish_blocks(
    half,
    grams,
    own_e,
    near_e,
    far_e,
    pivot1_ref,
    link_ref,
    pivot2_ref,
    parent_ref,
    one_ref,
    two_ref,
    out_diag,
    out_link,
    out_last,
    d_ref,
):
    own_a, near_a, far_a, own_b, near_b, far_b = grams
    my_row, my_col = lax.axis_index("prow"), lax.axis_index("pcol")
    y, k = my_row % 2, my_col % 2
    stays = k == y
    b1, b2 = link_ref.shape[1:]
    order = family_order(parent_ref, my_col)
    low = (my_row // 2) % 2
    for f, g_a, g_b, energy in (
        (1 - y, near_a[...], near_b[...], near_e[...]),
        (
            y,
            jnp.where(stays, own_a[...], far_a[...]),
            jnp.where(stays, own_b[...], far_b[...]),
            jnp.where(stays, own_e[...], far_e[...]),
        ),
    ):
        d_ref[pl.ds(pl.multiple_of(low * half, 8), half), :] = g_a
        d_ref[pl.ds(pl.multiple_of((1 - low) * half, 8), half), :] = g_b
        size = one_ref[my_col * 2 + f]
        diag = pivot1_ref[f] * below(size, (b1, b1), 0) * below(size, (b1, b1), 1) + d_ref[:, :b1]
        out_diag[f] = diag
        diag = halves(diag)
        for i in range(2):
            child = pick([order[i], order[2 + i]], f)
            width = two_ref[my_col * 4 + child]
            link = halves(link_ref[child] * below(size, (b1, b2), 0) * below(width, (b1, b2), 1))
            cross = d_ref[:, b1 + i * b2 : b1 + (i + 1) * b2]
            down = cross - dot3(diag, link, NN)
            out_link[child] = down
            pivot = pivot2_ref[child] * below(width, (b2, b2), 0) * below(width, (b2, b2), 1)
            out_last[child] = (
                pivot
                - dot3(link, halves(down), TN)
                - dot3(halves(cross), link, TN)
                + energy[:, i * b2 : (i + 1) * b2]
            )


def call(body, outs, ins, scratch=(), scalars=0, name=None, flops=0):
    specs = [VMEM] * (len(ins) - scalars) + [SMEM] * scalars
    moved = 4 * sum(v.size for v in ins) + sum(v.size * v.dtype.itemsize for v in outs)
    return pl.pallas_call(
        body,
        out_shape=outs,
        in_specs=specs,
        out_specs=[VMEM] * len(outs),
        scratch_shapes=list(scratch),
        name=name,
        compiler_params=pltpu.CompilerParams(vmem_limit_bytes=40 * 2**20),
        cost_estimate=pl.CostEstimate(flops=flops, bytes_accessed=moved, transcendentals=0),
    )(*ins)


def array(*shape, dtype=F32):
    return jax.ShapeDtypeStruct(shape, dtype)


def solution(mesh):
    rows_of, cols_of = mesh.shape["prow"], mesh.shape["pcol"]
    depth, wide = rows_of // 2, cols_of // 2

    def pairs(move):
        out = []
        for z in range(depth):
            for y in range(2):
                for x in range(wide):
                    for k in range(2):
                        to = move(z, y, x, k)
                        if to is not None:
                            a, b, c, d = to
                            out.append(((z * 2 + y) * cols_of + x * 2 + k, (a * 2 + b) * cols_of + c * 2 + d))
        return out

    to_worker = pairs(lambda z, y, x, k: (z, y, x, 1 - k) if k == y else (z, 1 - y, x, k))
    to_home = pairs(lambda z, y, x, k: (z, 1 - y, x, k) if k == y else (z, y, x, 1 - k))
    across = pairs(lambda z, y, x, k: None if k == y else (z, 1 - y, x, 1 - k))
    other_y = pairs(lambda z, y, x, k: (z, 1 - y, x, k))
    other_core = pairs(lambda z, y, x, k: (z, y, x, 1 - k))
    up = pairs(lambda z, y, x, k: (z + 1, y, x, k) if z + 1 < depth else None)
    down = pairs(lambda z, y, x, k: (z - 1, y, x, k) if z > 0 else None)

    def send(value, perm):
        return lax.ppermute(value, AXES, perm)

    def on_device(
        anc_inverse,
        factor_one,
        pivot_one,
        factor_two,
        factor_link,
        pivot_two,
        pattern_one,
        pattern_two,
        parent_two,
        size_one,
        size_two,
    ):
        rows, tile = anc_inverse.shape
        total = tile * cols_of
        span = 2 * rows
        b1, b2 = pivot_one.shape[1], pivot_two.shape[1]
        z = lax.axis_index("prow") // 2
        block = array(b1, rows)
        kept1, give1 = call(
            functools.partial(pack_one, b1), [block] * 2, [factor_one, pattern_one, size_one], scalars=2, name="pack_one"
        )
        near1, far1 = send(give1, to_worker), send(kept1, across)
        beside = send(anc_inverse, other_y)
        tiles = [[anc_inverse, beside]]
        for s in range(1, wide):
            turn = pairs(lambda z, y, x, k: (z, y, (x + s) % wide, k))
            tiles.append([send(anc_inverse, turn), send(beside, turn)])
        kept2, give2 = call(
            functools.partial(pack_two, b2),
            [block] * 2,
            [factor_two, pattern_one, pattern_two, parent_two, size_two],
            scalars=4,
            name="pack_two",
        )
        near2, far2 = send(give2, to_worker), send(kept2, across)
        (w1,) = call(join, [array(b1, span)], [kept1, near1, far1], name="join_one")
        (w2,) = call(join, [array(b1, span)], [kept2, near2, far2], name="join_two")
        panel = []
        for mine in tiles:
            panel += mine + [send(v, other_core) for v in mine]
        parts, high, low = call(
            functools.partial(partial_products, wide),
            [array(b1, total), array(span, total, dtype=jnp.bfloat16), array(span, total, dtype=jnp.bfloat16)],
            [w2] + panel,
            name="partial_products",
            flops=6 * b1 * span * total,
        )

        def combined(s, from_below, from_above):
            whole = pl.BlockSpec((b1, span), lambda i, at: (0, 0))
            spec = pltpu.PrefetchScalarGridSpec(
                num_scalar_prefetch=1,
                grid=(1,),
                in_specs=[
                    whole,
                    whole,
                    pl.BlockSpec((b1, span), lambda i, at: (0, jnp.minimum(at[0] + 1 + depth - s, depth - 1))),
                    pl.BlockSpec((b1, span), lambda i, at: (0, jnp.maximum(at[0] - 1 - depth + s, 0))),
                ],
                out_specs=[whole, whole],
            )

            def body(at_ref, *refs):
                combine(depth, s, *refs)

            return pl.pallas_call(body, grid_spec=spec, out_shape=[array(b1, span)] * 2, name="combine")(
                z[None], from_below, from_above, parts, parts
            )

        from_below = from_above = w1
        taken = []
        for s in range(1, depth + 1):
            go_up, go_down = (w1, w1) if s == 1 else combined(s, from_below, from_above)
            from_below, from_above = send(go_up, up), send(go_down, down)
            if s < depth:
                taken += [from_below, from_above]
        half = b1 // 2
        same1, other1, give1, mine, theirs = call(
            functools.partial(gram_products, depth),
            [block] * 3 + [array(half, 2 * b1)] * 2,
            [high, low, w1, w2] + taken,
            scratch=[pltpu.VMEM((b1, span), F32)],
            name="gram_products",
            flops=6 * b1 * span * total,
        )
        home1 = [same1, send(give1, to_home), send(other1, across)]

        def swap(value, step):
            return send(value, pairs(lambda z, y, x, k: (z ^ step, y, x, k)))

        def deliver(value):
            return [value, send(value, to_home), send(value, across)]

        grams = mine + swap(theirs, 1)
        step = 2
        while step < depth:
            grams = grams + swap(grams, step)
            step *= 2
        grams_a = deliver(grams)
        grams_b = deliver(swap(grams, 1))

        def last_part():
            whole = pl.BlockSpec((b1, span), lambda i, at: (0, 0))
            small = pl.BlockSpec((b1, rows), lambda i, at: (0, 0))
            spec = pltpu.PrefetchScalarGridSpec(
                num_scalar_prefetch=1,
                grid=(1,),
                in_specs=[pl.BlockSpec((b1, span), lambda i, at: (0, at[0])), whole, whole, whole],
                out_specs=[small] * 3 + [pl.BlockSpec((b2, 2 * b2), lambda i, at: (0, 0))],
            )

            def body(at_ref, *refs):
                energy_products(*refs)

            return pl.pallas_call(body, grid_spec=spec, out_shape=[block] * 3 + [array(b2, 2 * b2)], name="energy")(
                z[None], parts, from_below, from_above, w2
            )

        same2, other2, give2, energy = last_part()
        home2 = [same2, send(give2, to_home), send(other2, across)]
        step = 1
        while step < depth:
            energy = energy + swap(energy, step)
            step *= 2
        energies = deliver(energy)
        scalars = [pattern_one, pattern_two, parent_two, size_one, size_two]
        inverse_one, inverse_two = call(
            finish_rows,
            [array(rows, 2 * b1), array(rows, 4 * b2)],
            home1 + home2 + [factor_link] + scalars,
            scalars=5,
            name="finish_rows",
        )

        def blocks_body(*refs):
            finish_blocks(half, refs[:6], *refs[6:])

        diagonal_one, inverse_link, diagonal_two = call(
            blocks_body,
            [array(*pivot_one.shape), array(*factor_link.shape), array(*pivot_two.shape)],
            grams_a + grams_b + energies + [pivot_one, factor_link, pivot_two] + scalars[2:],
            scratch=[pltpu.VMEM((b1, 2 * b1), F32)],
            scalars=3,
            name="finish_blocks",
        )
        return inverse_one, diagonal_one, inverse_two, inverse_link, diagonal_two

    return jax.shard_map(
        on_device,
        mesh=mesh,
        in_specs=(
            P("prow", "pcol"),
            P("prow", "pcol"),
            P("pcol", None, None),
            P("prow", "pcol"),
            P("pcol", None, None),
            P("pcol", None, None),
            P(),
            P(),
            P(),
            P(),
            P(),
        ),
        out_specs=(
            P("prow", "pcol"),
            P("pcol", None, None),
            P("prow", "pcol"),
            P("pcol", None, None),
            P("pcol", None, None),
        ),
        check_vma=False,
    )
```

```python
import functools

import jax
import jax.numpy as jnp
from jax import lax
from jax.experimental import pallas as pl
from jax.experimental.pallas import tpu as pltpu
from jax.sharding import PartitionSpec as P

AXES = ("prow", "pcol")
CHUNKS = 2
LAG = 0
OPT = {'CHUNKS': 2, 'LAG': 0, 'merge': 1, 'w2': 3, 'wtie': 1, 'relay': 4, 'half': 1, 'one': 1, 'gram': 0, 'early': 1, 'ztwo': 1, 'zone': 2, 'home': 0}
FREE = pl.CostEstimate(flops=0, bytes_accessed=0, transcendentals=0)
F32 = jnp.float32
VMEM = pl.BlockSpec(memory_space=pltpu.VMEM)
SMEM = pl.BlockSpec(memory_space=pltpu.SMEM)
NN = ((1,), (0,))
NT = ((1,), (1,))
TN = ((0,), (0,))


def halves(value):
    high = value.astype(jnp.bfloat16)
    return high, (value - high.astype(F32)).astype(jnp.bfloat16)


def dot3(left, right, dims):
    def one(a, b):
        return lax.dot_general(a, b, (dims, ((), ())), preferred_element_type=F32)

    return one(left[0], right[0]) + (one(left[0], right[1]) + one(left[1], right[0]))


def place_of():
    my_row, my_col = lax.axis_index("prow"), lax.axis_index("pcol")
    return my_row // 2, my_row % 2, my_col // 2, my_col % 2


def family_order(parent_ref, my_col):
    parents = [parent_ref[my_col * 4 + i] - my_col * 2 for i in range(4)]
    place = []
    for i in range(4):
        seen = jnp.int32(0)
        for j in range(i):
            seen += jnp.where(parents[j] == parents[i], 1, 0)
        place.append(2 * parents[i] + seen)
    order = []
    for j in range(4):
        found = jnp.int32(0)
        for i in range(1, 4):
            found += jnp.where(place[i] == j, i, 0)
        order.append(found)
    return order


def below(size, shape, axis):
    return (lax.broadcasted_iota(jnp.int32, shape, axis) < size).astype(F32)


def pick(values, index):
    out = values[0]
    for i in range(1, len(values)):
        out = jnp.where(index == i, values[i], out)
    return out


def pack_one(factor_ref, first_ref, size_ref, kept_ref, give_ref):
    my_row, my_col = lax.axis_index("prow"), lax.axis_index("pcol")
    y = my_row % 2
    for out_ref, f in ((kept_ref, y), (give_ref, 1 - y)):
        block = out_ref.shape[0]
        values = factor_ref[:, pl.ds(pl.multiple_of(f * block, 128), block)]
        on = first_ref[my_row, my_col * 2 + f].astype(F32)
        keep = below(size_ref[my_col * 2 + f], values.shape, 1) * on
        out_ref[...] = (values * keep).T


def pack_two(factor_ref, first_ref, second_ref, parent_ref, size_ref, kept_ref, give_ref):
    my_row, my_col = lax.axis_index("prow"), lax.axis_index("pcol")
    y = my_row % 2
    order = family_order(parent_ref, my_col)
    for out_ref, f in ((kept_ref, y), (give_ref, 1 - y)):
        block = out_ref.shape[0] // 2
        for i in range(2):
            child = pick([order[i], order[2 + i]], f)
            values = factor_ref[:, pl.ds(pl.multiple_of(child * block, 128), block)]
            on = first_ref[my_row, my_col * 2 + f] * second_ref[my_row, my_col * 4 + child]
            keep = below(size_ref[my_col * 4 + child], values.shape, 1) * on.astype(F32)
            out_ref[i * block : (i + 1) * block, :] = (values * keep).T


def pack(one_ref, two_ref, first_ref, second_ref, parent_ref, size1_ref, size2_ref, kept_ref, give_ref):
    my_row, my_col = lax.axis_index("prow"), lax.axis_index("pcol")
    y = my_row % 2
    order = family_order(parent_ref, my_col)
    wide = kept_ref.shape[0] // 2
    block = wide // 2
    for out_ref, f in ((kept_ref, y), (give_ref, 1 - y)):
        values = one_ref[:, pl.ds(pl.multiple_of(f * wide, 128), wide)]
        on = first_ref[my_row, my_col * 2 + f]
        keep = below(size1_ref[my_col * 2 + f], values.shape, 1) * on.astype(F32)
        out_ref[:wide] = (values * keep).T
        for i in range(2):
            child = pick([order[i], order[2 + i]], f)
            values = two_ref[:, pl.ds(pl.multiple_of(child * block, 128), block)]
            both = (on * second_ref[my_row, my_col * 4 + child]).astype(F32)
            keep = below(size2_ref[my_col * 4 + child], values.shape, 1) * both
            out_ref[wide + i * block : wide + (i + 1) * block] = (values * keep).T


def join(kept_ref, near_ref, far_ref, *outs):
    _, y, _, k = place_of()
    rows = kept_ref.shape[1]
    for c, out_ref in enumerate(outs):
        cut = slice(c * out_ref.shape[0], (c + 1) * out_ref.shape[0])

        @pl.when(k == y)
        def _():
            out_ref[:, :rows] = kept_ref[cut, :]
            out_ref[:, rows:] = near_ref[cut, :]

        @pl.when(k != y)
        def _():
            out_ref[:, :rows] = near_ref[cut, :]
            out_ref[:, rows:] = far_ref[cut, :]


def partial_products(wide, counts, w2_ref, *refs):
    parts_ref, high_ref, low_ref = refs[-3:]
    _, y, x, k = place_of()
    rows, tile = refs[0].shape
    tiles, start = [], 0
    for count in counts:
        tiles.append(refs[start : start + count])
        start += count
    w2 = halves(w2_ref[...])
    same = (w2[0][:, :rows], w2[1][:, :rows])
    other = (w2[0][:, rows:], w2[1][:, rows:])
    for s in range(wide):
        for c in range(2):
            top, bottom = tiles[0][0], tiles[0][1:]
            del tiles[0]
            first = (lax.rem(x + wide - s, wide) * 2 + (k if c == 0 else 1 - k)) * (tile // rows)
            for b in range(tile // rows):
                block = first + b
                block = block - lax.rem(block, 2) + jnp.where(y == 0, lax.rem(block, 2), 1 - lax.rem(block, 2))
                at = pl.ds(pl.multiple_of(block * rows, 128), rows)
                cut = slice(b * rows, (b + 1) * rows)
                a = halves(top[:, cut])
                high_ref[:rows, at], low_ref[:rows, at] = a
                done = dot3(same, a, NN)
                a = halves(jnp.concatenate([ref[:, cut] for ref in bottom], axis=0))
                high_ref[rows:, at], low_ref[rows:, at] = a
                parts_ref[:, at] = done + dot3(other, a, NN)


def combine(depth, s, up_ref, down_ref, part_up_ref, part_down_ref, go_up_ref, go_down_ref):
    z = lax.axis_index("prow") // 2

    @pl.when(z <= s - 2 - LAG)
    def _():
        go_up_ref[...] = up_ref[...] + part_up_ref[...]

    @pl.when(z > s - 2 - LAG)
    def _():
        go_up_ref[...] = up_ref[...]

    @pl.when(depth - 1 - z <= s - 2 - LAG)
    def _():
        go_down_ref[...] = down_ref[...] + part_down_ref[...]

    @pl.when(depth - 1 - z > s - 2 - LAG)
    def _():
        go_down_ref[...] = down_ref[...]


def line_of(value):
    shape = value.shape
    same = lax.broadcasted_iota(jnp.int32, shape, 0) == lax.broadcasted_iota(jnp.int32, shape, 1)
    return jnp.sum(jnp.where(same, value, 0.0), axis=0, keepdims=True)


def fold(upper, lower):
    shape = upper.shape
    row, column = lax.broadcasted_iota(jnp.int32, shape, 0), lax.broadcasted_iota(jnp.int32, shape, 1)
    return jnp.where(row <= column, 0.5 * (upper + upper.T), 0.5 * (lower + lower.T))


def unfold(folded, line):
    shape = folded.shape
    row, column = lax.broadcasted_iota(jnp.int32, shape, 0), lax.broadcasted_iota(jnp.int32, shape, 1)
    turned = folded.T
    upper = jnp.where(row <= column, folded, turned)
    lower = jnp.where(row > column, folded, jnp.where(row < column, turned, line))
    return upper, lower


def all_rows(refs):
    return jnp.concatenate([ref[...] for ref in refs], axis=0)


def panel_product(high_ref, low_ref, value, at):
    span = value.shape[1]
    columns = pl.ds(pl.multiple_of(at * span, 128), span)
    return dot3(halves(value), (high_ref[:, columns], low_ref[:, columns]), NT)


def own_product(high_ref, low_ref, *refs):
    refs[-1][...] = panel_product(high_ref, low_ref, all_rows(refs[:-1]), lax.axis_index("prow") // 2)


def add_products(depth, s, out_ref, total, high_ref, low_ref, from_below, from_above):
    z = lax.axis_index("prow") // 2
    out_ref[...] = total

    @pl.when(z >= s)
    def _():
        out_ref[...] += panel_product(high_ref, low_ref, all_rows(from_below), z - s)

    @pl.when(z + s < depth)
    def _():
        out_ref[...] += panel_product(high_ref, low_ref, all_rows(from_above), z + s)


def next_product(depth, s, chunks, high_ref, low_ref, total_ref, *refs):
    add_products(depth, s, refs[-1], total_ref[...], high_ref, low_ref, refs[:chunks], refs[chunks : 2 * chunks])


def gram_products(depth, s, chunks, high_ref, low_ref, before_ref, *refs):
    taken = refs[: 2 * chunks]
    w1_ref, w2_ref, y1_ref, mine_ref, theirs_ref, total_ref = refs[2 * chunks :]
    z = lax.axis_index("prow") // 2
    add_products(depth, s, total_ref, before_ref[...], high_ref, low_ref, taken[:chunks], taken[chunks:])
    y1_ref[...] = total_ref[...]
    y1, w1, w2 = halves(total_ref[...]), halves(w1_ref[...]), halves(w2_ref[...])
    half = mine_ref.shape[1] // 3
    cross = dot3(y1, w2, NT)
    gram = dot3(w1, y1, NT)
    first = jnp.concatenate([cross[:half], fold(gram[:half, :half], gram[half:, half:])], axis=1)
    middle = 0.5 * (gram[:half, half:] + gram[half:, :half].T)
    second = jnp.concatenate([cross[half:], middle], axis=1)
    low = z % 2 == 0
    line = jnp.concatenate([jnp.zeros((8, 2 * half), F32), jnp.broadcast_to(line_of(gram[half:, half:]), (8, half))], axis=1)
    mine_ref[:half] = jnp.where(low, first, second)
    theirs_ref[:half] = jnp.where(low, second, first)
    mine_ref[half:] = line
    theirs_ref[half:] = line


def energy_products(chunks, part_ref, *refs):
    from_below, from_above, (w2_ref, y1_ref) = refs[:chunks], refs[chunks : 2 * chunks], refs[2 * chunks : 2 * chunks + 2]
    same_ref, other_ref, give_ref, energy_ref = refs[2 * chunks + 2 :]
    _, y, _, k = place_of()
    wide, rows = y1_ref.shape[0], y1_ref.shape[1] // 2
    y2 = part_ref[...] + (all_rows(from_below) + all_rows(from_above))
    for start, values in ((0, y1_ref[...]), (wide, y2)):
        same_ref[start : start + wide] = values[:, :rows]
        other_ref[start : start + wide] = values[:, rows:]
        give_ref[start : start + wide] = jnp.where(k == y, values[:, rows:], values[:, :rows])
    y2, w2 = halves(y2), halves(w2_ref[...])
    block = energy_ref.shape[1]
    own = []
    for i in range(2):
        cut = slice(i * block, (i + 1) * block)
        own.append(dot3((w2[0][cut], w2[1][cut]), (y2[0][cut], y2[1][cut]), NT))
    energy_ref[:block] = fold(*own)
    energy_ref[block:] = jnp.broadcast_to(line_of(own[1]), (8, block))


def collect(depth, grams_ref, other_ref, *refs):
    out_ref = refs[-1]
    half = grams_ref.shape[1]
    low = (lax.axis_index("prow") // 2) % 2 == 0
    out_ref[:, :half] = jnp.where(low, grams_ref[...], other_ref[...])
    out_ref[:, half : 2 * half] = jnp.where(low, other_ref[...], grams_ref[...])
    total = refs[0][...]
    for ref in refs[1:-1]:
        total = total + ref[...]
    out_ref[:, 2 * half :] = total


def finish_rows(
    own, near, far, link_ref, first_ref, second_ref, parent_ref, one_ref, two_ref, out1, out2
):
    my_row, my_col = lax.axis_index("prow"), lax.axis_index("pcol")
    y, k = my_row % 2, my_col % 2
    b1, b2 = link_ref.shape[1:]
    order = family_order(parent_ref, my_col)
    for f, both in ((1 - y, near[...]), (y, jnp.where(k == y, own[...], far[...]))):
        y1, y2 = both[:b1].T, both[b1:].T
        on = first_ref[my_row, my_col * 2 + f]
        out1[:, pl.ds(pl.multiple_of(f * b1, 128), b1)] = -y1 * on.astype(F32)
        y1 = halves(y1)
        for i in range(2):
            child = pick([order[i], order[2 + i]], f)
            link = (
                link_ref[child]
                * below(one_ref[my_col * 2 + f], (b1, b2), 0)
                * below(two_ref[my_col * 4 + child], (b1, b2), 1)
            )
            both = (on * second_ref[my_row, my_col * 4 + child]).astype(F32)
            near = dot3(y1, halves(link), NN)
            out2[:, pl.ds(pl.multiple_of(child * b2, 128), b2)] = (near - y2[:, i * b2 : (i + 1) * b2]) * both


def finish_blocks(
    own, near, far, pivot1_ref, link_ref, pivot2_ref, parent_ref, one_ref, two_ref, out_diag, out_link, out_last, d_ref
):
    my_row, my_col = lax.axis_index("prow"), lax.axis_index("pcol")
    y, k = my_row % 2, my_col % 2
    b1, b2 = link_ref.shape[1:]
    order = family_order(parent_ref, my_col)
    for f, sums in ((1 - y, near[...]), (y, jnp.where(k == y, own[...], far[...]))):
        line = sums[b2 : b2 + 1]
        sums = sums[:b2]
        upper, lower = unfold(sums[:, 2 * b2 : 3 * b2], line[:, 2 * b2 : 3 * b2])
        d_ref[:b2, :b2] = upper
        d_ref[:b2, b2:] = sums[:, 5 * b2 : 6 * b2]
        d_ref[b2:, :b2] = sums[:, 5 * b2 : 6 * b2].T
        d_ref[b2:, b2:] = lower
        energy = unfold(sums[:, 6 * b2 :], line[:, 6 * b2 :])
        crosses = jnp.concatenate([sums[:, : 2 * b2], sums[:, 3 * b2 : 5 * b2]], axis=0)
        size = one_ref[my_col * 2 + f]
        diag = pivot1_ref[f] * below(size, (b1, b1), 0) * below(size, (b1, b1), 1) + d_ref[...]
        out_diag[f] = diag
        diag = halves(diag)
        for i in range(2):
            child = pick([order[i], order[2 + i]], f)
            width = two_ref[my_col * 4 + child]
            link = halves(link_ref[child] * below(size, (b1, b2), 0) * below(width, (b1, b2), 1))
            cross = crosses[:, i * b2 : (i + 1) * b2]
            down = cross - dot3(diag, link, NN)
            out_link[child] = down
            pivot = pivot2_ref[child] * below(width, (b2, b2), 0) * below(width, (b2, b2), 1)
            out_last[child] = pivot - dot3(link, halves(down), TN) - dot3(halves(cross), link, TN) + energy[i]


def call(body, outs, ins, scratch=(), scalars=0, name=None, room=8):
    specs = [VMEM] * (len(ins) - scalars) + [SMEM] * scalars
    return pl.pallas_call(
        body,
        out_shape=outs,
        in_specs=specs,
        out_specs=[VMEM] * len(outs),
        scratch_shapes=list(scratch),
        name=name,
        compiler_params=pltpu.CompilerParams(vmem_limit_bytes=room * 2**20),
        cost_estimate=FREE,
    )(*ins)


def array(*shape, dtype=F32):
    return jax.ShapeDtypeStruct(shape, dtype)


def solution(mesh):
    rows_of, cols_of = mesh.shape["prow"], mesh.shape["pcol"]
    depth, wide = rows_of // 2, cols_of // 2

    def pairs(move):
        out = []
        for z in range(depth):
            for y in range(2):
                for x in range(wide):
                    for k in range(2):
                        to = move(z, y, x, k)
                        if to is not None:
                            a, b, c, d = to
                            out.append(((z * 2 + y) * cols_of + x * 2 + k, (a * 2 + b) * cols_of + c * 2 + d))
        return out

    to_worker = pairs(lambda z, y, x, k: (z, y, x, 1 - k) if k == y else (z, 1 - y, x, k))
    to_home = pairs(lambda z, y, x, k: (z, 1 - y, x, k) if k == y else (z, y, x, 1 - k))
    across = pairs(lambda z, y, x, k: None if k == y else (z, 1 - y, x, 1 - k))
    other_y = pairs(lambda z, y, x, k: (z, 1 - y, x, k))
    other_core = pairs(lambda z, y, x, k: (z, y, x, 1 - k))
    up = pairs(lambda z, y, x, k: (z + 1, y, x, k) if z + 1 < depth else None)
    down = pairs(lambda z, y, x, k: (z - 1, y, x, k) if z > 0 else None)

    def send(value, perm):
        return lax.ppermute(value, AXES, perm)

    def on_device(
        anc_inverse,
        factor_one,
        pivot_one,
        factor_two,
        factor_link,
        pivot_two,
        pattern_one,
        pattern_two,
        parent_two,
        size_one,
        size_two,
    ):
        rows, tile = anc_inverse.shape
        total = tile * cols_of
        span = 2 * rows
        b1, b2 = pivot_one.shape[1], pivot_two.shape[1]
        z = lax.axis_index("prow") // 2
        block = array(b1, rows)
        scalars = [pattern_one, pattern_two, parent_two, size_one, size_two]
        def tie(*values):
            return lax.optimization_barrier(values)

        piece = array(b1 // CHUNKS, span)
        beside = send(anc_inverse, other_y)
        turns = [pairs(lambda z, y, x, k: (z, y, (x + s) % wide, k)) for s in range(1, wide)]
        tops = [send(anc_inverse, turn) for turn in turns]
        if OPT["merge"]:
            kept, give = call(
                pack, [array(2 * b1, rows)] * 2, [factor_one, factor_two] + scalars, scalars=5, name="pack"
            )
            near, far = send(give, to_worker), send(kept, across)
            if OPT["wtie"]:
                near, far, beside = tie(near, far, beside)
            w1, w2 = call(join, [array(b1, span)] * 2, [kept, near, far], name="join")
            give1 = give
        else:
            kept1, give1 = call(pack_one, [block] * 2, [factor_one, pattern_one, size_one], scalars=2, name="pack_one")
            near1, far1 = send(give1, to_worker), send(kept1, across)
            if OPT["w2"] == 1:
                factor_two, _ = tie(factor_two, give1)
            if OPT["w2"] == 2:
                factor_two, near1, far1 = tie(factor_two, near1, far1)
            if OPT["w2"] == 3:
                factor_two, near1, far1, beside = tie(factor_two, near1, far1, beside)
            kept2, give2 = call(
                pack_two,
                [block] * 2,
                [factor_two, pattern_one, pattern_two, parent_two, size_two],
                scalars=4,
                name="pack_two",
            )
            if OPT["wtie"] == 1:
                near1, far1, kept2, give2 = tie(near1, far1, kept2, give2)
            if OPT["wtie"] == 2:
                near1, far1, beside = tie(near1, far1, beside)
            (w1,) = call(join, [array(b1, span)], [kept1, near1, far1], name="join_one")
            if OPT["wtie"] == 3:
                w1, kept2, give2 = tie(w1, kept2, give2)
            near2, far2 = send(give2, to_worker), send(kept2, across)
            if OPT["wtie"] == 4:
                near1, far1, near2, far2 = tie(near1, far1, near2, far2)
            (w2,) = call(join, [array(b1, span)], [kept2, near2, far2], name="join_two")
        passed = beside
        if OPT["relay"] == 1:
            passed, _ = tie(beside, give1)
        if OPT["relay"] == 2:
            passed, w1 = tie(beside, w1)
        if OPT["relay"] == 3:
            passed, _ = tie(beside, w1)
        if OPT["relay"] == 4:
            passed, w1, *tops = tie(beside, w1, *tops)
        middle = rows // 2
        tiles = [[anc_inverse, beside]]
        for turn, top in zip(turns, tops):
            if OPT["half"]:
                tiles.append([top, send(passed[:middle], turn), send(top[middle:], other_y)])
            else:
                tiles.append([top, send(passed, turn)])
        from_below, from_above = [send(w1, up)], [send(w1, down)]
        if OPT["one"] == 1:
            w2, from_below, from_above = tie(w2, from_below, from_above)
        if OPT["one"] == 2:
            tiles[1:], from_below, from_above = tie(tiles[1:], from_below, from_above)
        if OPT["one"] == 3:
            tiles[1][1], from_below, from_above = tie(tiles[1][1], from_below, from_above)
        panel = []
        for mine in tiles:
            panel += mine + [send(v, other_core) for v in mine]
        parts, high, low = call(
            functools.partial(partial_products, wide, [len(m) for m in tiles for _ in range(2)]),
            [array(b1, total), array(span, total, dtype=jnp.bfloat16), array(span, total, dtype=jnp.bfloat16)],
            [w2] + panel,
            name="partial_products",
            room=20,
        )

        def combined(s, c, from_below, from_above):
            whole = pl.BlockSpec(piece.shape, lambda i, at: (0, 0))
            taken = pl.BlockSpec(piece.shape, lambda i, at: (c if s == 2 + LAG else 0, 0))
            spec = pltpu.PrefetchScalarGridSpec(
                num_scalar_prefetch=1,
                grid=(1,),
                in_specs=[
                    taken,
                    taken,
                    pl.BlockSpec(piece.shape, lambda i, at: (c, jnp.clip(at[0] + 1 + depth + LAG - s, 0, depth - 1))),
                    pl.BlockSpec(piece.shape, lambda i, at: (c, jnp.clip(at[0] - 1 - depth - LAG + s, 0, depth - 1))),
                ],
                out_specs=[whole, whole],
            )

            def body(at_ref, *refs):
                combine(depth, s, *refs)

            return pl.pallas_call(
                body,
                grid_spec=spec,
                out_shape=[piece] * 2,
                name="combine",
                cost_estimate=FREE,
                compiler_params=pltpu.CompilerParams(vmem_limit_bytes=8 * 2**20),
            )(z[None], from_below, from_above, parts, parts)

        half = b1 // 2
        for s in range(1, depth + LAG):
            taken, chunks = from_below + from_above, len(from_below)
            blocks = range(1 if s <= LAG else CHUNKS)
            if s <= LAG:
                go = [(from_below[0], from_above[0])]
            else:
                go = [combined(s + 1, c, from_below[c % chunks], from_above[c % chunks]) for c in blocks]
            if s == depth - 1 and OPT["gram"] == 1:
                y1, go = tie(y1, go)
            if s == depth - 1 and OPT["gram"] == 2:
                y1, go[0] = tie(y1, go[0])
            from_below = [send(go[c][0], up) for c in blocks]
            from_above = [send(go[c][1], down) for c in blocks]
            if s == 1:
                (y1,) = call(own_product, [array(b1, span)], [high, low, w1], name="own_product", room=20)
            if s < depth - 1:
                (y1,) = call(
                    functools.partial(next_product, depth, s, chunks),
                    [array(b1, span)],
                    [high, low, y1] + taken,
                    name="next_product",
                    room=20,
                )
                if OPT["early"]:
                    y1, go = tie(y1, go)
            if s == depth - 1:
                y1, mine, theirs = call(
                    functools.partial(gram_products, depth, s, chunks),
                    [array(b1, span)] + [array(half + 8, 3 * half)] * 2,
                    [high, low, y1] + taken + [w1, w2],
                    scratch=[pltpu.VMEM((b1, span), F32)],
                    name="gram_products",
                    room=20,
                )

        def swap(value, step):
            return send(value, pairs(lambda z, y, x, k: (z ^ step, y, x, k)))

        def deliver(same, give, other):
            return [same, send(give, to_home), send(other, across)]

        grams = mine + swap(theirs, 1)
        if OPT["ztwo"]:
            grams, from_below[0], from_above[0] = tie(grams, from_below[0], from_above[0])
        step = 2
        while 2 * step < depth:
            grams = grams + swap(grams, step)
            step *= 2
        arrived = swap(grams, step)

        def last_part():
            whole = pl.BlockSpec((b1, span), lambda i, at: (0, 0))
            part = pl.BlockSpec(piece.shape, lambda i, at: (0, 0))
            small = pl.BlockSpec((2 * b1, rows), lambda i, at: (0, 0))
            spec = pltpu.PrefetchScalarGridSpec(
                num_scalar_prefetch=1,
                grid=(1,),
                in_specs=[pl.BlockSpec((b1, span), lambda i, at: (0, at[0]))] + [part] * (2 * CHUNKS) + [whole, whole],
                out_specs=[small] * 3 + [pl.BlockSpec((b2 + 8, b2), lambda i, at: (0, 0))],
            )

            def body(at_ref, *refs):
                energy_products(CHUNKS, *refs)

            return pl.pallas_call(
                body,
                grid_spec=spec,
                out_shape=[array(2 * b1, rows)] * 3 + [array(b2 + 8, b2)],
                name="energy",
                cost_estimate=FREE,
                compiler_params=pltpu.CompilerParams(vmem_limit_bytes=12 * 2**20),
            )(z[None], parts, *from_below, *from_above, w2, y1)

        same, other, give, energy = last_part()
        home = deliver(same, give, other)
        if OPT["zone"] == 2:
            arrived, energy = tie(arrived, energy)
        step = 1
        while 2 * step < depth:
            energy = energy + swap(energy, step)
            step *= 2
        if OPT["zone"] == 1:
            arrived, energy = tie(arrived, energy)
        grams = grams + arrived
        grams_too = swap(grams, 1)
        energies = [energy, swap(energy, step)]
        if OPT["home"] == 1:
            grams_too, home = tie(grams_too, home)
        if OPT["home"] == 2:
            grams, home = tie(grams, home)
        (sums,) = call(
            functools.partial(collect, depth), [array(half + 8, 7 * half)], [grams, grams_too] + energies, name="collect"
        )
        sums = deliver(sums, sums, sums)
        inverse_one, inverse_two = call(
            finish_rows,
            [array(rows, 2 * b1), array(rows, 4 * b2)],
            home + [factor_link] + scalars,
            scalars=5,
            name="finish_rows",
            room=16,
        )

        diagonal_one, inverse_link, diagonal_two = call(
            finish_blocks,
            [array(*pivot_one.shape), array(*factor_link.shape), array(*pivot_two.shape)],
            sums + [pivot_one, factor_link, pivot_two] + scalars[2:],
            scratch=[pltpu.VMEM((b1, b1), F32)],
            scalars=3,
            name="finish_blocks",
            room=16,
        )
        return inverse_one, diagonal_one, inverse_two, inverse_link, diagonal_two

    return jax.shard_map(
        on_device,
        mesh=mesh,
        in_specs=(
            P("prow", "pcol"),
            P("prow", "pcol"),
            P("pcol", None, None),
            P("prow", "pcol"),
            P("pcol", None, None),
            P("pcol", None, None),
            P(),
            P(),
            P(),
            P(),
            P(),
        ),
        out_specs=(
            P("prow", "pcol"),
            P("pcol", None, None),
            P("prow", "pcol"),
            P("pcol", None, None),
            P("pcol", None, None),
        ),
        check_vma=False,
    )
```

```python
import functools

import jax
import jax.numpy as jnp
from jax import lax
from jax.experimental import pallas as pl
from jax.experimental.pallas import tpu as pltpu
from jax.sharding import PartitionSpec as P

AXES = ("prow", "pcol")
CHUNKS = 2
FREE = pl.CostEstimate(flops=0, bytes_accessed=0, transcendentals=0)
F32 = jnp.float32
VMEM = pl.BlockSpec(memory_space=pltpu.VMEM)
SMEM = pl.BlockSpec(memory_space=pltpu.SMEM)
NN = ((1,), (0,))
NT = ((1,), (1,))
TN = ((0,), (0,))


def halves(value):
    high = value.astype(jnp.bfloat16)
    return high, (value - high.astype(F32)).astype(jnp.bfloat16)


def dot3(left, right, dims):
    def one(a, b):
        return lax.dot_general(a, b, (dims, ((), ())), preferred_element_type=F32)

    return one(left[0], right[0]) + (one(left[0], right[1]) + one(left[1], right[0]))


def place_of():
    my_row, my_col = lax.axis_index("prow"), lax.axis_index("pcol")
    return my_row // 2, my_row % 2, my_col // 2, my_col % 2


def family_order(parent_ref, my_col):
    parents = [parent_ref[my_col * 4 + i] - my_col * 2 for i in range(4)]
    place = []
    for i in range(4):
        seen = jnp.int32(0)
        for j in range(i):
            seen += jnp.where(parents[j] == parents[i], 1, 0)
        place.append(2 * parents[i] + seen)
    order = []
    for j in range(4):
        found = jnp.int32(0)
        for i in range(1, 4):
            found += jnp.where(place[i] == j, i, 0)
        order.append(found)
    return order


def below(size, shape, axis):
    return (lax.broadcasted_iota(jnp.int32, shape, axis) < size).astype(F32)


def pick(values, index):
    out = values[0]
    for i in range(1, len(values)):
        out = jnp.where(index == i, values[i], out)
    return out


def pack_one(factor_ref, first_ref, size_ref, kept_ref, give_ref):
    my_row, my_col = lax.axis_index("prow"), lax.axis_index("pcol")
    y = my_row % 2
    for out_ref, f in ((kept_ref, y), (give_ref, 1 - y)):
        block = out_ref.shape[0]
        values = factor_ref[:, pl.ds(pl.multiple_of(f * block, 128), block)]
        on = first_ref[my_row, my_col * 2 + f].astype(F32)
        keep = below(size_ref[my_col * 2 + f], values.shape, 1) * on
        out_ref[...] = (values * keep).T


def pack_two(factor_ref, first_ref, second_ref, parent_ref, size_ref, kept_ref, give_ref):
    my_row, my_col = lax.axis_index("prow"), lax.axis_index("pcol")
    y = my_row % 2
    order = family_order(parent_ref, my_col)
    for out_ref, f in ((kept_ref, y), (give_ref, 1 - y)):
        block = out_ref.shape[0] // 2
        for i in range(2):
            child = pick([order[i], order[2 + i]], f)
            values = factor_ref[:, pl.ds(pl.multiple_of(child * block, 128), block)]
            on = first_ref[my_row, my_col * 2 + f] * second_ref[my_row, my_col * 4 + child]
            keep = below(size_ref[my_col * 4 + child], values.shape, 1) * on.astype(F32)
            out_ref[i * block : (i + 1) * block, :] = (values * keep).T


def join(kept_ref, near_ref, far_ref, *outs):
    _, y, _, k = place_of()
    rows = kept_ref.shape[1]
    for c, out_ref in enumerate(outs):
        cut = slice(c * out_ref.shape[0], (c + 1) * out_ref.shape[0])

        @pl.when(k == y)
        def _():
            out_ref[:, :rows] = kept_ref[cut, :]
            out_ref[:, rows:] = near_ref[cut, :]

        @pl.when(k != y)
        def _():
            out_ref[:, :rows] = near_ref[cut, :]
            out_ref[:, rows:] = far_ref[cut, :]


def partial_products(wide, counts, w2_ref, *refs):
    parts_ref, high_ref, low_ref = refs[-3:]
    _, y, x, k = place_of()
    rows, tile = refs[0].shape
    tiles, start = [], 0
    for count in counts:
        tiles.append(refs[start : start + count])
        start += count
    w2 = halves(w2_ref[...])
    same = (w2[0][:, :rows], w2[1][:, :rows])
    other = (w2[0][:, rows:], w2[1][:, rows:])
    for s in range(wide):
        for c in range(2):
            top, bottom = tiles[0][0], tiles[0][1:]
            del tiles[0]
            first = (lax.rem(x + wide - s, wide) * 2 + (k if c == 0 else 1 - k)) * (tile // rows)
            for b in range(tile // rows):
                block = first + b
                block = block - lax.rem(block, 2) + jnp.where(y == 0, lax.rem(block, 2), 1 - lax.rem(block, 2))
                at = pl.ds(pl.multiple_of(block * rows, 128), rows)
                cut = slice(b * rows, (b + 1) * rows)
                a = halves(top[:, cut])
                high_ref[:rows, at], low_ref[:rows, at] = a
                done = dot3(same, a, NN)
                a = halves(jnp.concatenate([ref[:, cut] for ref in bottom], axis=0))
                high_ref[rows:, at], low_ref[rows:, at] = a
                parts_ref[:, at] = done + dot3(other, a, NN)


def combine(depth, s, up_ref, down_ref, part_up_ref, part_down_ref, go_up_ref, go_down_ref):
    z = lax.axis_index("prow") // 2

    @pl.when(z <= s - 2)
    def _():
        go_up_ref[...] = up_ref[...] + part_up_ref[...]

    @pl.when(z > s - 2)
    def _():
        go_up_ref[...] = up_ref[...]

    @pl.when(depth - 1 - z <= s - 2)
    def _():
        go_down_ref[...] = down_ref[...] + part_down_ref[...]

    @pl.when(depth - 1 - z > s - 2)
    def _():
        go_down_ref[...] = down_ref[...]


def line_of(value):
    shape = value.shape
    same = lax.broadcasted_iota(jnp.int32, shape, 0) == lax.broadcasted_iota(jnp.int32, shape, 1)
    return jnp.sum(jnp.where(same, value, 0.0), axis=0, keepdims=True)


def fold(upper, lower):
    shape = upper.shape
    row, column = lax.broadcasted_iota(jnp.int32, shape, 0), lax.broadcasted_iota(jnp.int32, shape, 1)
    return jnp.where(row <= column, 0.5 * (upper + upper.T), 0.5 * (lower + lower.T))


def unfold(folded, line):
    shape = folded.shape
    row, column = lax.broadcasted_iota(jnp.int32, shape, 0), lax.broadcasted_iota(jnp.int32, shape, 1)
    turned = folded.T
    upper = jnp.where(row <= column, folded, turned)
    lower = jnp.where(row > column, folded, jnp.where(row < column, turned, line))
    return upper, lower


def all_rows(refs):
    return jnp.concatenate([ref[...] for ref in refs], axis=0)


def panel_product(high_ref, low_ref, value, at):
    span = value.shape[1]
    columns = pl.ds(pl.multiple_of(at * span, 128), span)
    return dot3(halves(value), (high_ref[:, columns], low_ref[:, columns]), NT)


def own_product(high_ref, low_ref, *refs):
    refs[-1][...] = panel_product(high_ref, low_ref, all_rows(refs[:-1]), lax.axis_index("prow") // 2)


def add_products(depth, s, out_ref, total, high_ref, low_ref, from_below, from_above):
    z = lax.axis_index("prow") // 2
    out_ref[...] = total

    @pl.when(z >= s)
    def _():
        out_ref[...] += panel_product(high_ref, low_ref, all_rows(from_below), z - s)

    @pl.when(z + s < depth)
    def _():
        out_ref[...] += panel_product(high_ref, low_ref, all_rows(from_above), z + s)


def next_product(depth, s, chunks, high_ref, low_ref, total_ref, *refs):
    add_products(depth, s, refs[-1], total_ref[...], high_ref, low_ref, refs[:chunks], refs[chunks : 2 * chunks])


def gram_products(depth, s, chunks, high_ref, low_ref, before_ref, *refs):
    taken = refs[: 2 * chunks]
    w1_ref, w2_ref, y1_ref, mine_ref, theirs_ref, total_ref = refs[2 * chunks :]
    z = lax.axis_index("prow") // 2
    add_products(depth, s, total_ref, before_ref[...], high_ref, low_ref, taken[:chunks], taken[chunks:])
    y1_ref[...] = total_ref[...]
    y1, w1, w2 = halves(total_ref[...]), halves(w1_ref[...]), halves(w2_ref[...])
    half = mine_ref.shape[1] // 3
    cross = dot3(y1, w2, NT)
    gram = dot3(w1, y1, NT)
    first = jnp.concatenate([cross[:half], fold(gram[:half, :half], gram[half:, half:])], axis=1)
    middle = 0.5 * (gram[:half, half:] + gram[half:, :half].T)
    second = jnp.concatenate([cross[half:], middle], axis=1)
    low = z % 2 == 0
    line = jnp.concatenate([jnp.zeros((8, 2 * half), F32), jnp.broadcast_to(line_of(gram[half:, half:]), (8, half))], axis=1)
    mine_ref[:half] = jnp.where(low, first, second)
    theirs_ref[:half] = jnp.where(low, second, first)
    mine_ref[half:] = line
    theirs_ref[half:] = line


def energy_products(chunks, part_ref, *refs):
    from_below, from_above, (w2_ref, y1_ref) = refs[:chunks], refs[chunks : 2 * chunks], refs[2 * chunks : 2 * chunks + 2]
    same_ref, other_ref, give_ref, energy_ref = refs[2 * chunks + 2 :]
    _, y, _, k = place_of()
    wide, rows = y1_ref.shape[0], y1_ref.shape[1] // 2
    y2 = part_ref[...] + (all_rows(from_below) + all_rows(from_above))
    for start, values in ((0, y1_ref[...]), (wide, y2)):
        same_ref[start : start + wide] = values[:, :rows]
        other_ref[start : start + wide] = values[:, rows:]
        give_ref[start : start + wide] = jnp.where(k == y, values[:, rows:], values[:, :rows])
    y2, w2 = halves(y2), halves(w2_ref[...])
    block = energy_ref.shape[1]
    own = []
    for i in range(2):
        cut = slice(i * block, (i + 1) * block)
        own.append(dot3((w2[0][cut], w2[1][cut]), (y2[0][cut], y2[1][cut]), NT))
    energy_ref[:block] = fold(*own)
    energy_ref[block:] = jnp.broadcast_to(line_of(own[1]), (8, block))


def collect(depth, grams_ref, other_ref, *refs):
    out_ref = refs[-1]
    half = grams_ref.shape[1]
    low = (lax.axis_index("prow") // 2) % 2 == 0
    out_ref[:, :half] = jnp.where(low, grams_ref[...], other_ref[...])
    out_ref[:, half : 2 * half] = jnp.where(low, other_ref[...], grams_ref[...])
    total = refs[0][...]
    for ref in refs[1:-1]:
        total = total + ref[...]
    out_ref[:, 2 * half :] = total


def finish_rows(
    own, near, far, link_ref, first_ref, second_ref, parent_ref, one_ref, two_ref, out1, out2
):
    my_row, my_col = lax.axis_index("prow"), lax.axis_index("pcol")
    y, k = my_row % 2, my_col % 2
    b1, b2 = link_ref.shape[1:]
    order = family_order(parent_ref, my_col)
    for f, both in ((1 - y, near[...]), (y, jnp.where(k == y, own[...], far[...]))):
        y1, y2 = both[:b1].T, both[b1:].T
        on = first_ref[my_row, my_col * 2 + f]
        out1[:, pl.ds(pl.multiple_of(f * b1, 128), b1)] = -y1 * on.astype(F32)
        y1 = halves(y1)
        for i in range(2):
            child = pick([order[i], order[2 + i]], f)
            link = (
                link_ref[child]
                * below(one_ref[my_col * 2 + f], (b1, b2), 0)
                * below(two_ref[my_col * 4 + child], (b1, b2), 1)
            )
            both = (on * second_ref[my_row, my_col * 4 + child]).astype(F32)
            near = dot3(y1, halves(link), NN)
            out2[:, pl.ds(pl.multiple_of(child * b2, 128), b2)] = (near - y2[:, i * b2 : (i + 1) * b2]) * both


def finish_blocks(
    own, near, far, pivot1_ref, link_ref, pivot2_ref, parent_ref, one_ref, two_ref, out_diag, out_link, out_last, d_ref
):
    my_row, my_col = lax.axis_index("prow"), lax.axis_index("pcol")
    y, k = my_row % 2, my_col % 2
    b1, b2 = link_ref.shape[1:]
    order = family_order(parent_ref, my_col)
    for f, sums in ((1 - y, near[...]), (y, jnp.where(k == y, own[...], far[...]))):
        line = sums[b2 : b2 + 1]
        sums = sums[:b2]
        upper, lower = unfold(sums[:, 2 * b2 : 3 * b2], line[:, 2 * b2 : 3 * b2])
        d_ref[:b2, :b2] = upper
        d_ref[:b2, b2:] = sums[:, 5 * b2 : 6 * b2]
        d_ref[b2:, :b2] = sums[:, 5 * b2 : 6 * b2].T
        d_ref[b2:, b2:] = lower
        energy = unfold(sums[:, 6 * b2 :], line[:, 6 * b2 :])
        crosses = jnp.concatenate([sums[:, : 2 * b2], sums[:, 3 * b2 : 5 * b2]], axis=0)
        size = one_ref[my_col * 2 + f]
        diag = pivot1_ref[f] * below(size, (b1, b1), 0) * below(size, (b1, b1), 1) + d_ref[...]
        out_diag[f] = diag
        diag = halves(diag)
        for i in range(2):
            child = pick([order[i], order[2 + i]], f)
            width = two_ref[my_col * 4 + child]
            link = halves(link_ref[child] * below(size, (b1, b2), 0) * below(width, (b1, b2), 1))
            cross = crosses[:, i * b2 : (i + 1) * b2]
            down = cross - dot3(diag, link, NN)
            out_link[child] = down
            pivot = pivot2_ref[child] * below(width, (b2, b2), 0) * below(width, (b2, b2), 1)
            out_last[child] = pivot - dot3(link, halves(down), TN) - dot3(halves(cross), link, TN) + energy[i]


def call(body, outs, ins, scratch=(), scalars=0, name=None, room=8):
    specs = [VMEM] * (len(ins) - scalars) + [SMEM] * scalars
    return pl.pallas_call(
        body,
        out_shape=outs,
        in_specs=specs,
        out_specs=[VMEM] * len(outs),
        scratch_shapes=list(scratch),
        name=name,
        compiler_params=pltpu.CompilerParams(vmem_limit_bytes=room * 2**20),
        cost_estimate=FREE,
    )(*ins)


def array(*shape, dtype=F32):
    return jax.ShapeDtypeStruct(shape, dtype)


def solution(mesh):
    rows_of, cols_of = mesh.shape["prow"], mesh.shape["pcol"]
    depth, wide = rows_of // 2, cols_of // 2

    def pairs(move):
        out = []
        for z in range(depth):
            for y in range(2):
                for x in range(wide):
                    for k in range(2):
                        to = move(z, y, x, k)
                        if to is not None:
                            a, b, c, d = to
                            out.append(((z * 2 + y) * cols_of + x * 2 + k, (a * 2 + b) * cols_of + c * 2 + d))
        return out

    to_worker = pairs(lambda z, y, x, k: (z, y, x, 1 - k) if k == y else (z, 1 - y, x, k))
    to_home = pairs(lambda z, y, x, k: (z, 1 - y, x, k) if k == y else (z, y, x, 1 - k))
    across = pairs(lambda z, y, x, k: None if k == y else (z, 1 - y, x, 1 - k))
    other_y = pairs(lambda z, y, x, k: (z, 1 - y, x, k))
    other_core = pairs(lambda z, y, x, k: (z, y, x, 1 - k))
    up = pairs(lambda z, y, x, k: (z + 1, y, x, k) if z + 1 < depth else None)
    down = pairs(lambda z, y, x, k: (z - 1, y, x, k) if z > 0 else None)

    def send(value, perm):
        return lax.ppermute(value, AXES, perm)

    def on_device(
        anc_inverse,
        factor_one,
        pivot_one,
        factor_two,
        factor_link,
        pivot_two,
        pattern_one,
        pattern_two,
        parent_two,
        size_one,
        size_two,
    ):
        rows, tile = anc_inverse.shape
        total = tile * cols_of
        span = 2 * rows
        b1, b2 = pivot_one.shape[1], pivot_two.shape[1]
        z = lax.axis_index("prow") // 2
        block = array(b1, rows)
        scalars = [pattern_one, pattern_two, parent_two, size_one, size_two]

        def tie(*values):
            return lax.optimization_barrier(values)

        piece = array(b1 // CHUNKS, span)
        beside = send(anc_inverse, other_y)
        turns = [pairs(lambda z, y, x, k: (z, y, (x + s) % wide, k)) for s in range(1, wide)]
        tops = [send(anc_inverse, turn) for turn in turns]
        beside, *tops = tie(beside, *tops)
        kept1, give1 = call(pack_one, [block] * 2, [factor_one, pattern_one, size_one], scalars=2, name="pack_one")
        near1, far1 = send(give1, to_worker), send(kept1, across)
        factor_two, near1, far1 = tie(factor_two, near1, far1)
        kept2, give2 = call(
            pack_two,
            [block] * 2,
            [factor_two, pattern_one, pattern_two, parent_two, size_two],
            scalars=4,
            name="pack_two",
        )
        near1, far1, kept2, give2 = tie(near1, far1, kept2, give2)
        (w1,) = call(join, [array(b1, span)], [kept1, near1, far1], name="join_one")
        near2, far2 = send(give2, to_worker), send(kept2, across)
        (w2,) = call(join, [array(b1, span)], [kept2, near2, far2], name="join_two")
        passed, _ = tie(beside, w1)
        middle = rows // 2
        tiles = [[anc_inverse, beside]]
        for turn, top in zip(turns, tops):
            tiles.append([top, send(passed[:middle], turn), send(top[middle:], other_y)])
        from_below, from_above = [send(w1, up)], [send(w1, down)]
        w2, from_below, from_above = tie(w2, from_below, from_above)
        panel = []
        for mine in tiles:
            panel += mine + [send(v, other_core) for v in mine]
        parts, high, low = call(
            functools.partial(partial_products, wide, [len(m) for m in tiles for _ in range(2)]),
            [array(b1, total), array(span, total, dtype=jnp.bfloat16), array(span, total, dtype=jnp.bfloat16)],
            [w2] + panel,
            name="partial_products",
            room=20,
        )

        def combined(s, c, from_below, from_above):
            whole = pl.BlockSpec(piece.shape, lambda i, at: (0, 0))
            taken = pl.BlockSpec(piece.shape, lambda i, at: (c if s == 2 else 0, 0))
            spec = pltpu.PrefetchScalarGridSpec(
                num_scalar_prefetch=1,
                grid=(1,),
                in_specs=[
                    taken,
                    taken,
                    pl.BlockSpec(piece.shape, lambda i, at: (c, jnp.clip(at[0] + 1 + depth - s, 0, depth - 1))),
                    pl.BlockSpec(piece.shape, lambda i, at: (c, jnp.clip(at[0] - 1 - depth + s, 0, depth - 1))),
                ],
                out_specs=[whole, whole],
            )

            def body(at_ref, *refs):
                combine(depth, s, *refs)

            return pl.pallas_call(
                body,
                grid_spec=spec,
                out_shape=[piece] * 2,
                name="combine",
                cost_estimate=FREE,
                compiler_params=pltpu.CompilerParams(vmem_limit_bytes=8 * 2**20),
            )(z[None], from_below, from_above, parts, parts)

        half = b1 // 2
        for s in range(1, depth):
            taken, chunks = from_below + from_above, len(from_below)
            blocks = range(CHUNKS)
            go = [combined(s + 1, c, from_below[c % chunks], from_above[c % chunks]) for c in blocks]
            from_below = [send(go[c][0], up) for c in blocks]
            from_above = [send(go[c][1], down) for c in blocks]
            if s == 1:
                (y1,) = call(own_product, [array(b1, span)], [high, low, w1], name="own_product", room=20)
            if s < depth - 1:
                (y1,) = call(
                    functools.partial(next_product, depth, s, chunks),
                    [array(b1, span)],
                    [high, low, y1] + taken,
                    name="next_product",
                    room=20,
                )
            if s == depth - 1:
                y1, mine, theirs = call(
                    functools.partial(gram_products, depth, s, chunks),
                    [array(b1, span)] + [array(half + 8, 3 * half)] * 2,
                    [high, low, y1] + taken + [w1, w2],
                    scratch=[pltpu.VMEM((b1, span), F32)],
                    name="gram_products",
                    room=20,
                )

        def swap(value, step):
            return send(value, pairs(lambda z, y, x, k: (z ^ step, y, x, k)))

        def deliver(same, give, other):
            return [same, send(give, to_home), send(other, across)]

        grams = mine + swap(theirs, 1)
        grams, from_below[0], from_above[0] = tie(grams, from_below[0], from_above[0])
        step = 2
        while 2 * step < depth:
            grams = grams + swap(grams, step)
            step *= 2
        arrived = swap(grams, step)

        def last_part():
            whole = pl.BlockSpec((b1, span), lambda i, at: (0, 0))
            part = pl.BlockSpec(piece.shape, lambda i, at: (0, 0))
            small = pl.BlockSpec((2 * b1, rows), lambda i, at: (0, 0))
            spec = pltpu.PrefetchScalarGridSpec(
                num_scalar_prefetch=1,
                grid=(1,),
                in_specs=[pl.BlockSpec((b1, span), lambda i, at: (0, at[0]))] + [part] * (2 * CHUNKS) + [whole, whole],
                out_specs=[small] * 3 + [pl.BlockSpec((b2 + 8, b2), lambda i, at: (0, 0))],
            )

            def body(at_ref, *refs):
                energy_products(CHUNKS, *refs)

            return pl.pallas_call(
                body,
                grid_spec=spec,
                out_shape=[array(2 * b1, rows)] * 3 + [array(b2 + 8, b2)],
                name="energy",
                cost_estimate=FREE,
                compiler_params=pltpu.CompilerParams(vmem_limit_bytes=12 * 2**20),
            )(z[None], parts, *from_below, *from_above, w2, y1)

        same, other, give, energy = last_part()
        home = deliver(same, give, other)
        step = 1
        while 2 * step < depth:
            energy = energy + swap(energy, step)
            step *= 2
        arrived, energy = tie(arrived, energy)
        grams = grams + arrived
        grams_too = swap(grams, 1)
        energies = [energy, swap(energy, step)]
        (sums,) = call(
            functools.partial(collect, depth), [array(half + 8, 7 * half)], [grams, grams_too] + energies, name="collect"
        )
        sums = deliver(sums, sums, sums)
        inverse_one, inverse_two = call(
            finish_rows,
            [array(rows, 2 * b1), array(rows, 4 * b2)],
            home + [factor_link] + scalars,
            scalars=5,
            name="finish_rows",
            room=16,
        )

        diagonal_one, inverse_link, diagonal_two = call(
            finish_blocks,
            [array(*pivot_one.shape), array(*factor_link.shape), array(*pivot_two.shape)],
            sums + [pivot_one, factor_link, pivot_two] + scalars[2:],
            scratch=[pltpu.VMEM((b1, b1), F32)],
            scalars=3,
            name="finish_blocks",
            room=16,
        )
        return inverse_one, diagonal_one, inverse_two, inverse_link, diagonal_two

    return jax.shard_map(
        on_device,
        mesh=mesh,
        in_specs=(
            P("prow", "pcol"),
            P("prow", "pcol"),
            P("pcol", None, None),
            P("prow", "pcol"),
            P("pcol", None, None),
            P("pcol", None, None),
            P(),
            P(),
            P(),
            P(),
            P(),
        ),
        out_specs=(
            P("prow", "pcol"),
            P("pcol", None, None),
            P("prow", "pcol"),
            P("pcol", None, None),
            P("pcol", None, None),
        ),
        check_vma=False,
    )
```

```python
import functools

import jax
import jax.numpy as jnp
from jax import lax
from jax.experimental import pallas as pl
from jax.experimental.pallas import tpu as pltpu
from jax.sharding import PartitionSpec as P

AXES = ("prow", "pcol")
CHUNKS = 2
FREE = pl.CostEstimate(flops=0, bytes_accessed=0, transcendentals=0)
F32 = jnp.float32
VMEM = pl.BlockSpec(memory_space=pltpu.VMEM)
SMEM = pl.BlockSpec(memory_space=pltpu.SMEM)
NN = ((1,), (0,))
NT = ((1,), (1,))
TN = ((0,), (0,))


def halves(value):
    high = value.astype(jnp.bfloat16)
    return high, (value - high.astype(F32)).astype(jnp.bfloat16)


def dot3(left, right, dims):
    def one(a, b):
        return lax.dot_general(a, b, (dims, ((), ())), preferred_element_type=F32)

    return one(left[0], right[0]) + (one(left[0], right[1]) + one(left[1], right[0]))


def place_of():
    my_row, my_col = lax.axis_index("prow"), lax.axis_index("pcol")
    return my_row // 2, my_row % 2, my_col // 2, my_col % 2


def family_order(parent_ref, my_col):
    parents = [parent_ref[my_col * 4 + i] - my_col * 2 for i in range(4)]
    place = []
    for i in range(4):
        seen = jnp.int32(0)
        for j in range(i):
            seen += jnp.where(parents[j] == parents[i], 1, 0)
        place.append(2 * parents[i] + seen)
    order = []
    for j in range(4):
        found = jnp.int32(0)
        for i in range(1, 4):
            found += jnp.where(place[i] == j, i, 0)
        order.append(found)
    return order


def below(size, shape, axis):
    return (lax.broadcasted_iota(jnp.int32, shape, axis) < size).astype(F32)


def pick(values, index):
    out = values[0]
    for i in range(1, len(values)):
        out = jnp.where(index == i, values[i], out)
    return out


def pack_one(factor_ref, first_ref, size_ref, kept_ref, give_ref):
    my_row, my_col = lax.axis_index("prow"), lax.axis_index("pcol")
    y = my_row % 2
    for out_ref, f in ((kept_ref, y), (give_ref, 1 - y)):
        block = out_ref.shape[0]
        values = factor_ref[:, pl.ds(pl.multiple_of(f * block, 128), block)]
        on = first_ref[my_row, my_col * 2 + f].astype(F32)
        keep = below(size_ref[my_col * 2 + f], values.shape, 1) * on
        out_ref[...] = (values * keep).T


def pack_two(factor_ref, first_ref, second_ref, parent_ref, size_ref, kept_ref, give_ref):
    my_row, my_col = lax.axis_index("prow"), lax.axis_index("pcol")
    y = my_row % 2
    order = family_order(parent_ref, my_col)
    for out_ref, f in ((kept_ref, y), (give_ref, 1 - y)):
        block = out_ref.shape[0] // 2
        for i in range(2):
            child = pick([order[i], order[2 + i]], f)
            values = factor_ref[:, pl.ds(pl.multiple_of(child * block, 128), block)]
            on = first_ref[my_row, my_col * 2 + f] * second_ref[my_row, my_col * 4 + child]
            keep = below(size_ref[my_col * 4 + child], values.shape, 1) * on.astype(F32)
            out_ref[i * block : (i + 1) * block, :] = (values * keep).T


def join(kept_ref, near_ref, far_ref, *outs):
    _, y, _, k = place_of()
    rows = kept_ref.shape[1]
    for c, out_ref in enumerate(outs):
        cut = slice(c * out_ref.shape[0], (c + 1) * out_ref.shape[0])

        @pl.when(k == y)
        def _():
            out_ref[:, :rows] = kept_ref[cut, :]
            out_ref[:, rows:] = near_ref[cut, :]

        @pl.when(k != y)
        def _():
            out_ref[:, :rows] = near_ref[cut, :]
            out_ref[:, rows:] = far_ref[cut, :]


def partial_products(wide, counts, w2_ref, *refs):
    parts_ref, high_ref, low_ref = refs[-3:]
    _, y, x, k = place_of()
    rows, tile = refs[0].shape
    tiles, start = [], 0
    for count in counts:
        tiles.append(refs[start : start + count])
        start += count
    w2 = halves(w2_ref[...])
    same = (w2[0][:, :rows], w2[1][:, :rows])
    other = (w2[0][:, rows:], w2[1][:, rows:])
    for s in range(wide):
        for c in range(2):
            top, bottom = tiles[0][0], tiles[0][1:]
            del tiles[0]
            first = (lax.rem(x + wide - s, wide) * 2 + (k if c == 0 else 1 - k)) * (tile // rows)
            for b in range(tile // rows):
                block = first + b
                block = block - lax.rem(block, 2) + jnp.where(y == 0, lax.rem(block, 2), 1 - lax.rem(block, 2))
                at = pl.ds(pl.multiple_of(block * rows, 128), rows)
                cut = slice(b * rows, (b + 1) * rows)
                a = halves(top[:, cut])
                high_ref[:rows, at], low_ref[:rows, at] = a
                done = dot3(same, a, NN)
                a = halves(jnp.concatenate([ref[:, cut] for ref in bottom], axis=0))
                high_ref[rows:, at], low_ref[rows:, at] = a
                parts_ref[:, at] = done + dot3(other, a, NN)


def combine(depth, s, up_ref, down_ref, part_up_ref, part_down_ref, go_up_ref, go_down_ref):
    z = lax.axis_index("prow") // 2

    @pl.when(z <= s - 2)
    def _():
        go_up_ref[...] = up_ref[...] + part_up_ref[...]

    @pl.when(z > s - 2)
    def _():
        go_up_ref[...] = up_ref[...]

    @pl.when(depth - 1 - z <= s - 2)
    def _():
        go_down_ref[...] = down_ref[...] + part_down_ref[...]

    @pl.when(depth - 1 - z > s - 2)
    def _():
        go_down_ref[...] = down_ref[...]


def line_of(value):
    shape = value.shape
    same = lax.broadcasted_iota(jnp.int32, shape, 0) == lax.broadcasted_iota(jnp.int32, shape, 1)
    return jnp.sum(jnp.where(same, value, 0.0), axis=0, keepdims=True)


def fold(upper, lower):
    shape = upper.shape
    row, column = lax.broadcasted_iota(jnp.int32, shape, 0), lax.broadcasted_iota(jnp.int32, shape, 1)
    return jnp.where(row <= column, 0.5 * (upper + upper.T), 0.5 * (lower + lower.T))


def unfold(folded, line):
    shape = folded.shape
    row, column = lax.broadcasted_iota(jnp.int32, shape, 0), lax.broadcasted_iota(jnp.int32, shape, 1)
    turned = folded.T
    upper = jnp.where(row <= column, folded, turned)
    lower = jnp.where(row > column, folded, jnp.where(row < column, turned, line))
    return upper, lower


def all_rows(refs):
    return jnp.concatenate([ref[...] for ref in refs], axis=0)


def panel_product(high_ref, low_ref, value, at):
    span = value.shape[1]
    columns = pl.ds(pl.multiple_of(at * span, 128), span)
    return dot3(halves(value), (high_ref[:, columns], low_ref[:, columns]), NT)


def own_product(high_ref, low_ref, *refs):
    refs[-1][...] = panel_product(high_ref, low_ref, all_rows(refs[:-1]), lax.axis_index("prow") // 2)


def add_products(depth, s, out_ref, total, high_ref, low_ref, from_below, from_above):
    z = lax.axis_index("prow") // 2
    out_ref[...] = total

    @pl.when(z >= s)
    def _():
        out_ref[...] += panel_product(high_ref, low_ref, all_rows(from_below), z - s)

    @pl.when(z + s < depth)
    def _():
        out_ref[...] += panel_product(high_ref, low_ref, all_rows(from_above), z + s)


def next_product(depth, s, chunks, high_ref, low_ref, total_ref, *refs):
    add_products(depth, s, refs[-1], total_ref[...], high_ref, low_ref, refs[:chunks], refs[chunks : 2 * chunks])


def gram_products(depth, s, chunks, high_ref, low_ref, before_ref, *refs):
    taken = refs[: 2 * chunks]
    w1_ref, w2_ref, y1_ref, mine_ref, theirs_ref, total_ref = refs[2 * chunks :]
    z = lax.axis_index("prow") // 2
    add_products(depth, s, total_ref, before_ref[...], high_ref, low_ref, taken[:chunks], taken[chunks:])
    y1_ref[...] = total_ref[...]
    y1, w1, w2 = halves(total_ref[...]), halves(w1_ref[...]), halves(w2_ref[...])
    half = mine_ref.shape[1] // 3
    cross = dot3(y1, w2, NT)
    gram = dot3(w1, y1, NT)
    first = jnp.concatenate([cross[:half], fold(gram[:half, :half], gram[half:, half:])], axis=1)
    middle = 0.5 * (gram[:half, half:] + gram[half:, :half].T)
    second = jnp.concatenate([cross[half:], middle], axis=1)
    low = z % 2 == 0
    line = jnp.concatenate([jnp.zeros((8, 2 * half), F32), jnp.broadcast_to(line_of(gram[half:, half:]), (8, half))], axis=1)
    mine_ref[:half] = jnp.where(low, first, second)
    theirs_ref[:half] = jnp.where(low, second, first)
    mine_ref[half:] = line
    theirs_ref[half:] = line


def energy_products(chunks, part_ref, *refs):
    from_below, from_above, (w2_ref, y1_ref) = refs[:chunks], refs[chunks : 2 * chunks], refs[2 * chunks : 2 * chunks + 2]
    same_ref, other_ref, give_ref, energy_ref = refs[2 * chunks + 2 :]
    _, y, _, k = place_of()
    wide, rows = y1_ref.shape[0], y1_ref.shape[1] // 2
    y2 = part_ref[...] + (all_rows(from_below) + all_rows(from_above))
    for start, values in ((0, y1_ref[...]), (wide, y2)):
        same_ref[start : start + wide] = values[:, :rows]
        other_ref[start : start + wide] = values[:, rows:]
        give_ref[start : start + wide] = jnp.where(k == y, values[:, rows:], values[:, :rows])
    y2, w2 = halves(y2), halves(w2_ref[...])
    block = energy_ref.shape[1]
    own = []
    for i in range(2):
        cut = slice(i * block, (i + 1) * block)
        own.append(dot3((w2[0][cut], w2[1][cut]), (y2[0][cut], y2[1][cut]), NT))
    energy_ref[:block] = fold(*own)
    energy_ref[block:] = jnp.broadcast_to(line_of(own[1]), (8, block))


def collect(depth, grams_ref, other_ref, *refs):
    out_ref = refs[-1]
    half = grams_ref.shape[1]
    low = (lax.axis_index("prow") // 2) % 2 == 0
    out_ref[:, :half] = jnp.where(low, grams_ref[...], other_ref[...])
    out_ref[:, half : 2 * half] = jnp.where(low, other_ref[...], grams_ref[...])
    total = refs[0][...]
    for ref in refs[1:-1]:
        total = total + ref[...]
    out_ref[:, 2 * half :] = total


def finish_rows(
    own, near, far, link_ref, first_ref, second_ref, parent_ref, one_ref, two_ref, out1, out2
):
    my_row, my_col = lax.axis_index("prow"), lax.axis_index("pcol")
    y, k = my_row % 2, my_col % 2
    b1, b2 = link_ref.shape[1:]
    order = family_order(parent_ref, my_col)
    for f, both in ((1 - y, near[...]), (y, jnp.where(k == y, own[...], far[...]))):
        y1, y2 = both[:b1].T, both[b1:].T
        on = first_ref[my_row, my_col * 2 + f]
        out1[:, pl.ds(pl.multiple_of(f * b1, 128), b1)] = -y1 * on.astype(F32)
        y1 = halves(y1)
        for i in range(2):
            child = pick([order[i], order[2 + i]], f)
            link = (
                link_ref[child]
                * below(one_ref[my_col * 2 + f], (b1, b2), 0)
                * below(two_ref[my_col * 4 + child], (b1, b2), 1)
            )
            both = (on * second_ref[my_row, my_col * 4 + child]).astype(F32)
            near = dot3(y1, halves(link), NN)
            out2[:, pl.ds(pl.multiple_of(child * b2, 128), b2)] = (near - y2[:, i * b2 : (i + 1) * b2]) * both


def finish_blocks(
    own, near, far, pivot1_ref, link_ref, pivot2_ref, parent_ref, one_ref, two_ref, out_diag, out_link, out_last, d_ref
):
    my_row, my_col = lax.axis_index("prow"), lax.axis_index("pcol")
    y, k = my_row % 2, my_col % 2
    b1, b2 = link_ref.shape[1:]
    order = family_order(parent_ref, my_col)
    for f, sums in ((1 - y, near[...]), (y, jnp.where(k == y, own[...], far[...]))):
        line = sums[b2 : b2 + 1]
        sums = sums[:b2]
        upper, lower = unfold(sums[:, 2 * b2 : 3 * b2], line[:, 2 * b2 : 3 * b2])
        d_ref[:b2, :b2] = upper
        d_ref[:b2, b2:] = sums[:, 5 * b2 : 6 * b2]
        d_ref[b2:, :b2] = sums[:, 5 * b2 : 6 * b2].T
        d_ref[b2:, b2:] = lower
        energy = unfold(sums[:, 6 * b2 :], line[:, 6 * b2 :])
        crosses = jnp.concatenate([sums[:, : 2 * b2], sums[:, 3 * b2 : 5 * b2]], axis=0)
        size = one_ref[my_col * 2 + f]
        diag = pivot1_ref[f] * below(size, (b1, b1), 0) * below(size, (b1, b1), 1) + d_ref[...]
        out_diag[f] = diag
        diag = halves(diag)
        for i in range(2):
            child = pick([order[i], order[2 + i]], f)
            width = two_ref[my_col * 4 + child]
            link = halves(link_ref[child] * below(size, (b1, b2), 0) * below(width, (b1, b2), 1))
            cross = crosses[:, i * b2 : (i + 1) * b2]
            down = cross - dot3(diag, link, NN)
            out_link[child] = down
            pivot = pivot2_ref[child] * below(width, (b2, b2), 0) * below(width, (b2, b2), 1)
            out_last[child] = pivot - dot3(link, halves(down), TN) - dot3(halves(cross), link, TN) + energy[i]


def call(body, outs, ins, scratch=(), scalars=0, name=None, room=8):
    specs = [VMEM] * (len(ins) - scalars) + [SMEM] * scalars
    return pl.pallas_call(
        body,
        out_shape=outs,
        in_specs=specs,
        out_specs=[VMEM] * len(outs),
        scratch_shapes=list(scratch),
        name=name,
        compiler_params=pltpu.CompilerParams(vmem_limit_bytes=room * 2**20),
        cost_estimate=FREE,
    )(*ins)


def array(*shape, dtype=F32):
    return jax.ShapeDtypeStruct(shape, dtype)


def solution(mesh):
    rows_of, cols_of = mesh.shape["prow"], mesh.shape["pcol"]
    depth, wide = rows_of // 2, cols_of // 2

    def pairs(move):
        out = []
        for z in range(depth):
            for y in range(2):
                for x in range(wide):
                    for k in range(2):
                        to = move(z, y, x, k)
                        if to is not None:
                            a, b, c, d = to
                            out.append(((z * 2 + y) * cols_of + x * 2 + k, (a * 2 + b) * cols_of + c * 2 + d))
        return out

    to_worker = pairs(lambda z, y, x, k: (z, y, x, 1 - k) if k == y else (z, 1 - y, x, k))
    to_home = pairs(lambda z, y, x, k: (z, 1 - y, x, k) if k == y else (z, y, x, 1 - k))
    across = pairs(lambda z, y, x, k: None if k == y else (z, 1 - y, x, 1 - k))
    other_y = pairs(lambda z, y, x, k: (z, 1 - y, x, k))
    other_core = pairs(lambda z, y, x, k: (z, y, x, 1 - k))
    up = pairs(lambda z, y, x, k: (z + 1, y, x, k) if z + 1 < depth else None)
    down = pairs(lambda z, y, x, k: (z - 1, y, x, k) if z > 0 else None)

    def send(value, perm):
        return lax.ppermute(value, AXES, perm)

    def on_device(
        anc_inverse,
        factor_one,
        pivot_one,
        factor_two,
        factor_link,
        pivot_two,
        pattern_one,
        pattern_two,
        parent_two,
        size_one,
        size_two,
    ):
        rows, tile = anc_inverse.shape
        total = tile * cols_of
        span = 2 * rows
        b1, b2 = pivot_one.shape[1], pivot_two.shape[1]
        z = lax.axis_index("prow") // 2
        block = array(b1, rows)
        scalars = [pattern_one, pattern_two, parent_two, size_one, size_two]

        def tie(*values):
            return lax.optimization_barrier(values)

        piece = array(b1 // CHUNKS, span)
        turns = [pairs(lambda z, y, x, k: (z, y, (x + s) % wide, k)) for s in range(1, wide)]
        tops = [send(anc_inverse, turn) for turn in turns]
        beside = send(anc_inverse, other_y)
        beside, *tops = tie(beside, *tops)
        kept1, give1 = call(pack_one, [block] * 2, [factor_one, pattern_one, size_one], scalars=2, name="pack_one")
        near1, far1 = send(give1, to_worker), send(kept1, across)
        factor_two, near1, far1 = tie(factor_two, near1, far1)
        kept2, give2 = call(
            pack_two,
            [block] * 2,
            [factor_two, pattern_one, pattern_two, parent_two, size_two],
            scalars=4,
            name="pack_two",
        )
        near1, far1, kept2, give2 = tie(near1, far1, kept2, give2)
        (w1,) = call(join, [array(b1, span)], [kept1, near1, far1], name="join_one")
        near2, far2 = send(give2, to_worker), send(kept2, across)
        (w2,) = call(join, [array(b1, span)], [kept2, near2, far2], name="join_two")
        passed, _ = tie(beside, w1)
        middle = rows * 5 // 64 * 8
        tiles = [[anc_inverse, beside]]
        for turn, top in zip(turns, tops):
            tiles.append([top, send(passed[:middle], turn), send(top[middle:], other_y)])
        from_below, from_above = [send(w1, up)], [send(w1, down)]
        w2, from_below, from_above = tie(w2, from_below, from_above)
        panel = []
        for mine in tiles:
            panel += mine + [send(v, other_core) for v in mine]
        parts, high, low = call(
            functools.partial(partial_products, wide, [len(m) for m in tiles for _ in range(2)]),
            [array(b1, total), array(span, total, dtype=jnp.bfloat16), array(span, total, dtype=jnp.bfloat16)],
            [w2] + panel,
            name="partial_products",
            room=20,
        )

        def combined(s, c, from_below, from_above):
            whole = pl.BlockSpec(piece.shape, lambda i, at: (0, 0))
            taken = pl.BlockSpec(piece.shape, lambda i, at: (c if s == 2 else 0, 0))
            spec = pltpu.PrefetchScalarGridSpec(
                num_scalar_prefetch=1,
                grid=(1,),
                in_specs=[
                    taken,
                    taken,
                    pl.BlockSpec(piece.shape, lambda i, at: (c, jnp.clip(at[0] + 1 + depth - s, 0, depth - 1))),
                    pl.BlockSpec(piece.shape, lambda i, at: (c, jnp.clip(at[0] - 1 - depth + s, 0, depth - 1))),
                ],
                out_specs=[whole, whole],
            )

            def body(at_ref, *refs):
                combine(depth, s, *refs)

            return pl.pallas_call(
                body,
                grid_spec=spec,
                out_shape=[piece] * 2,
                name="combine",
                cost_estimate=FREE,
                compiler_params=pltpu.CompilerParams(vmem_limit_bytes=8 * 2**20),
            )(z[None], from_below, from_above, parts, parts)

        half = b1 // 2
        for s in range(1, depth):
            taken, chunks = from_below + from_above, len(from_below)
            blocks = range(CHUNKS)
            go = [combined(s + 1, c, from_below[c % chunks], from_above[c % chunks]) for c in blocks]
            from_below = [send(go[c][0], up) for c in blocks]
            from_above = [send(go[c][1], down) for c in blocks]
            if s == 1:
                (y1,) = call(own_product, [array(b1, span)], [high, low, w1], name="own_product", room=20)
            if s < depth - 1:
                (y1,) = call(
                    functools.partial(next_product, depth, s, chunks),
                    [array(b1, span)],
                    [high, low, y1] + taken,
                    name="next_product",
                    room=20,
                )
            if s == depth - 1:
                y1, mine, theirs = call(
                    functools.partial(gram_products, depth, s, chunks),
                    [array(b1, span)] + [array(half + 8, 3 * half)] * 2,
                    [high, low, y1] + taken + [w1, w2],
                    scratch=[pltpu.VMEM((b1, span), F32)],
                    name="gram_products",
                    room=20,
                )

        def swap(value, step):
            return send(value, pairs(lambda z, y, x, k: (z ^ step, y, x, k)))

        def deliver(same, give, other):
            return [same, send(give, to_home), send(other, across)]

        grams = mine + swap(theirs, 1)
        grams, from_below[0], from_above[0] = tie(grams, from_below[0], from_above[0])
        step = 2
        while 2 * step < depth:
            grams = grams + swap(grams, step)
            step *= 2
        arrived = swap(grams, step)

        def last_part():
            whole = pl.BlockSpec((b1, span), lambda i, at: (0, 0))
            part = pl.BlockSpec(piece.shape, lambda i, at: (0, 0))
            small = pl.BlockSpec((2 * b1, rows), lambda i, at: (0, 0))
            spec = pltpu.PrefetchScalarGridSpec(
                num_scalar_prefetch=1,
                grid=(1,),
                in_specs=[pl.BlockSpec((b1, span), lambda i, at: (0, at[0]))] + [part] * (2 * CHUNKS) + [whole, whole],
                out_specs=[small] * 3 + [pl.BlockSpec((b2 + 8, b2), lambda i, at: (0, 0))],
            )

            def body(at_ref, *refs):
                energy_products(CHUNKS, *refs)

            return pl.pallas_call(
                body,
                grid_spec=spec,
                out_shape=[array(2 * b1, rows)] * 3 + [array(b2 + 8, b2)],
                name="energy",
                cost_estimate=FREE,
                compiler_params=pltpu.CompilerParams(vmem_limit_bytes=12 * 2**20),
            )(z[None], parts, *from_below, *from_above, w2, y1)

        same, other, give, energy = last_part()
        home = deliver(same, give, other)
        step = 1
        while 2 * step < depth:
            energy = energy + swap(energy, step)
            step *= 2
        arrived, _ = tie(arrived, energy)
        grams = grams + arrived
        grams_too = swap(grams, 1)
        energies = [energy, swap(energy, step)]
        (sums,) = call(
            functools.partial(collect, depth), [array(half + 8, 7 * half)], [grams, grams_too] + energies, name="collect"
        )
        sums = deliver(sums, sums, sums)
        inverse_one, inverse_two = call(
            finish_rows,
            [array(rows, 2 * b1), array(rows, 4 * b2)],
            home + [factor_link] + scalars,
            scalars=5,
            name="finish_rows",
            room=16,
        )

        diagonal_one, inverse_link, diagonal_two = call(
            finish_blocks,
            [array(*pivot_one.shape), array(*factor_link.shape), array(*pivot_two.shape)],
            sums + [pivot_one, factor_link, pivot_two] + scalars[2:],
            scratch=[pltpu.VMEM((b1, b1), F32)],
            scalars=3,
            name="finish_blocks",
            room=16,
        )
        return inverse_one, diagonal_one, inverse_two, inverse_link, diagonal_two

    return jax.shard_map(
        on_device,
        mesh=mesh,
        in_specs=(
            P("prow", "pcol"),
            P("prow", "pcol"),
            P("pcol", None, None),
            P("prow", "pcol"),
            P("pcol", None, None),
            P("pcol", None, None),
            P(),
            P(),
            P(),
            P(),
            P(),
        ),
        out_specs=(
            P("prow", "pcol"),
            P("pcol", None, None),
            P("prow", "pcol"),
            P("pcol", None, None),
            P("pcol", None, None),
        ),
        check_vma=False,
    )
```

```python
import functools

import jax
import jax.numpy as jnp
from jax import lax
from jax.experimental import pallas as pl
from jax.experimental.pallas import tpu as pltpu
from jax.sharding import PartitionSpec as P

AXES = ("prow", "pcol")
CHUNKS = 2
FREE = pl.CostEstimate(flops=0, bytes_accessed=0, transcendentals=0)
F32 = jnp.float32
VMEM = pl.BlockSpec(memory_space=pltpu.VMEM)
SMEM = pl.BlockSpec(memory_space=pltpu.SMEM)
NN = ((1,), (0,))
NT = ((1,), (1,))
TN = ((0,), (0,))


def halves(value):
    high = value.astype(jnp.bfloat16)
    return high, (value - high.astype(F32)).astype(jnp.bfloat16)


def dot3(left, right, dims):
    def one(a, b):
        return lax.dot_general(a, b, (dims, ((), ())), preferred_element_type=F32)

    return one(left[0], right[0]) + (one(left[0], right[1]) + one(left[1], right[0]))


def place_of():
    my_row, my_col = lax.axis_index("prow"), lax.axis_index("pcol")
    return my_row // 2, my_row % 2, my_col // 2, my_col % 2


def family_order(parent_ref, my_col):
    parents = [parent_ref[my_col * 4 + i] - my_col * 2 for i in range(4)]
    place = []
    for i in range(4):
        seen = jnp.int32(0)
        for j in range(i):
            seen += jnp.where(parents[j] == parents[i], 1, 0)
        place.append(2 * parents[i] + seen)
    order = []
    for j in range(4):
        found = jnp.int32(0)
        for i in range(1, 4):
            found += jnp.where(place[i] == j, i, 0)
        order.append(found)
    return order


def below(size, shape, axis):
    return (lax.broadcasted_iota(jnp.int32, shape, axis) < size).astype(F32)


def pick(values, index):
    out = values[0]
    for i in range(1, len(values)):
        out = jnp.where(index == i, values[i], out)
    return out


def pack_one(factor_ref, first_ref, size_ref, kept_ref, give_ref):
    my_row, my_col = lax.axis_index("prow"), lax.axis_index("pcol")
    y = my_row % 2
    for out_ref, f in ((kept_ref, y), (give_ref, 1 - y)):
        block = out_ref.shape[0]
        values = factor_ref[:, pl.ds(pl.multiple_of(f * block, 128), block)]
        on = first_ref[my_row, my_col * 2 + f].astype(F32)
        keep = below(size_ref[my_col * 2 + f], values.shape, 1) * on
        out_ref[...] = (values * keep).T


def pack_two(factor_ref, first_ref, second_ref, parent_ref, size_ref, kept_ref, give_ref):
    my_row, my_col = lax.axis_index("prow"), lax.axis_index("pcol")
    y = my_row % 2
    order = family_order(parent_ref, my_col)
    for out_ref, f in ((kept_ref, y), (give_ref, 1 - y)):
        block = out_ref.shape[0] // 2
        for i in range(2):
            child = pick([order[i], order[2 + i]], f)
            values = factor_ref[:, pl.ds(pl.multiple_of(child * block, 128), block)]
            on = first_ref[my_row, my_col * 2 + f] * second_ref[my_row, my_col * 4 + child]
            keep = below(size_ref[my_col * 4 + child], values.shape, 1) * on.astype(F32)
            out_ref[i * block : (i + 1) * block, :] = (values * keep).T


def join(kept_ref, near_ref, far_ref, *outs):
    _, y, _, k = place_of()
    rows = kept_ref.shape[1]
    for c, out_ref in enumerate(outs):
        cut = slice(c * out_ref.shape[0], (c + 1) * out_ref.shape[0])

        @pl.when(k == y)
        def _():
            out_ref[:, :rows] = kept_ref[cut, :]
            out_ref[:, rows:] = near_ref[cut, :]

        @pl.when(k != y)
        def _():
            out_ref[:, :rows] = near_ref[cut, :]
            out_ref[:, rows:] = far_ref[cut, :]


def partial_products(wide, counts, w2_ref, *refs):
    parts_ref, high_ref, low_ref = refs[-3:]
    _, y, x, k = place_of()
    rows, tile = refs[0].shape
    tiles, start = [], 0
    for count in counts:
        tiles.append(refs[start : start + count])
        start += count
    w2 = halves(w2_ref[...])
    same = (w2[0][:, :rows], w2[1][:, :rows])
    other = (w2[0][:, rows:], w2[1][:, rows:])
    for s in range(wide):
        for c in range(2):
            top, bottom = tiles[0][0], tiles[0][1:]
            del tiles[0]
            first = (lax.rem(x + wide - s, wide) * 2 + (k if c == 0 else 1 - k)) * (tile // rows)
            for b in range(tile // rows):
                block = first + b
                block = block - lax.rem(block, 2) + jnp.where(y == 0, lax.rem(block, 2), 1 - lax.rem(block, 2))
                at = pl.ds(pl.multiple_of(block * rows, 128), rows)
                cut = slice(b * rows, (b + 1) * rows)
                a = halves(top[:, cut])
                high_ref[:rows, at], low_ref[:rows, at] = a
                done = dot3(same, a, NN)
                a = halves(jnp.concatenate([ref[:, cut] for ref in bottom], axis=0))
                high_ref[rows:, at], low_ref[rows:, at] = a
                parts_ref[:, at] = done + dot3(other, a, NN)


def combine(depth, s, up_ref, down_ref, part_up_ref, part_down_ref, go_up_ref, go_down_ref):
    z = lax.axis_index("prow") // 2

    @pl.when(z <= s - 2)
    def _():
        go_up_ref[...] = up_ref[...] + part_up_ref[...]

    @pl.when(z > s - 2)
    def _():
        go_up_ref[...] = up_ref[...]

    @pl.when(depth - 1 - z <= s - 2)
    def _():
        go_down_ref[...] = down_ref[...] + part_down_ref[...]

    @pl.when(depth - 1 - z > s - 2)
    def _():
        go_down_ref[...] = down_ref[...]


def line_of(value):
    shape = value.shape
    same = lax.broadcasted_iota(jnp.int32, shape, 0) == lax.broadcasted_iota(jnp.int32, shape, 1)
    return jnp.sum(jnp.where(same, value, 0.0), axis=0, keepdims=True)


def fold(upper, lower):
    shape = upper.shape
    row, column = lax.broadcasted_iota(jnp.int32, shape, 0), lax.broadcasted_iota(jnp.int32, shape, 1)
    return jnp.where(row <= column, 0.5 * (upper + upper.T), 0.5 * (lower + lower.T))


def unfold(folded, line):
    shape = folded.shape
    row, column = lax.broadcasted_iota(jnp.int32, shape, 0), lax.broadcasted_iota(jnp.int32, shape, 1)
    turned = folded.T
    upper = jnp.where(row <= column, folded, turned)
    lower = jnp.where(row > column, folded, jnp.where(row < column, turned, line))
    return upper, lower


def all_rows(refs):
    return jnp.concatenate([ref[...] for ref in refs], axis=0)


def panel_product(high_ref, low_ref, value, at):
    span = value.shape[1]
    columns = pl.ds(pl.multiple_of(at * span, 128), span)
    return dot3(halves(value), (high_ref[:, columns], low_ref[:, columns]), NT)


def own_product(high_ref, low_ref, *refs):
    refs[-1][...] = panel_product(high_ref, low_ref, all_rows(refs[:-1]), lax.axis_index("prow") // 2)


def add_products(depth, s, out_ref, total, high_ref, low_ref, from_below, from_above):
    z = lax.axis_index("prow") // 2
    out_ref[...] = total

    @pl.when(z >= s)
    def _():
        out_ref[...] += panel_product(high_ref, low_ref, all_rows(from_below), z - s)

    @pl.when(z + s < depth)
    def _():
        out_ref[...] += panel_product(high_ref, low_ref, all_rows(from_above), z + s)


def next_product(depth, s, chunks, high_ref, low_ref, total_ref, *refs):
    add_products(depth, s, refs[-1], total_ref[...], high_ref, low_ref, refs[:chunks], refs[chunks : 2 * chunks])


def gram_products(depth, s, chunks, high_ref, low_ref, before_ref, *refs):
    taken = refs[: 2 * chunks]
    w1_ref, w2_ref, y1_ref, mine_ref, theirs_ref, total_ref = refs[2 * chunks :]
    z = lax.axis_index("prow") // 2
    add_products(depth, s, total_ref, before_ref[...], high_ref, low_ref, taken[:chunks], taken[chunks:])
    y1_ref[...] = total_ref[...]
    y1, w1, w2 = halves(total_ref[...]), halves(w1_ref[...]), halves(w2_ref[...])
    half = mine_ref.shape[1] // 3
    cross = dot3(y1, w2, NT)
    gram = dot3(w1, y1, NT)
    first = jnp.concatenate([cross[:half], fold(gram[:half, :half], gram[half:, half:])], axis=1)
    middle = 0.5 * (gram[:half, half:] + gram[half:, :half].T)
    second = jnp.concatenate([cross[half:], middle], axis=1)
    low = z % 2 == 0
    line = jnp.concatenate([jnp.zeros((8, 2 * half), F32), jnp.broadcast_to(line_of(gram[half:, half:]), (8, half))], axis=1)
    mine_ref[:half] = jnp.where(low, first, second)
    theirs_ref[:half] = jnp.where(low, second, first)
    mine_ref[half:] = line
    theirs_ref[half:] = line


def energy_products(chunks, part_ref, *refs):
    from_below, from_above, (w2_ref, y1_ref) = refs[:chunks], refs[chunks : 2 * chunks], refs[2 * chunks : 2 * chunks + 2]
    same_ref, other_ref, give_ref, energy_ref = refs[2 * chunks + 2 :]
    _, y, _, k = place_of()
    wide, rows = y1_ref.shape[0], y1_ref.shape[1] // 2
    y2 = part_ref[...] + (all_rows(from_below) + all_rows(from_above))
    for start, values in ((0, y1_ref[...]), (wide, y2)):
        same_ref[start : start + wide] = values[:, :rows]
        other_ref[start : start + wide] = values[:, rows:]
        give_ref[start : start + wide] = jnp.where(k == y, values[:, rows:], values[:, :rows])
    y2, w2 = halves(y2), halves(w2_ref[...])
    block = energy_ref.shape[1]
    own = []
    for i in range(2):
        cut = slice(i * block, (i + 1) * block)
        own.append(dot3((w2[0][cut], w2[1][cut]), (y2[0][cut], y2[1][cut]), NT))
    energy_ref[:block] = fold(*own)
    energy_ref[block:] = jnp.broadcast_to(line_of(own[1]), (8, block))


def collect(depth, grams_ref, other_ref, *refs):
    out_ref = refs[-1]
    half = grams_ref.shape[1]
    low = (lax.axis_index("prow") // 2) % 2 == 0
    out_ref[:, :half] = jnp.where(low, grams_ref[...], other_ref[...])
    out_ref[:, half : 2 * half] = jnp.where(low, other_ref[...], grams_ref[...])
    total = refs[0][...]
    for ref in refs[1:-1]:
        total = total + ref[...]
    out_ref[:, 2 * half :] = total


def finish_rows(
    own, near, far, link_ref, first_ref, second_ref, parent_ref, one_ref, two_ref, out1, out2
):
    my_row, my_col = lax.axis_index("prow"), lax.axis_index("pcol")
    y, k = my_row % 2, my_col % 2
    b1, b2 = link_ref.shape[1:]
    order = family_order(parent_ref, my_col)
    for f, both in ((1 - y, near[...]), (y, jnp.where(k == y, own[...], far[...]))):
        y1, y2 = both[:b1].T, both[b1:].T
        on = first_ref[my_row, my_col * 2 + f]
        out1[:, pl.ds(pl.multiple_of(f * b1, 128), b1)] = -y1 * on.astype(F32)
        y1 = halves(y1)
        for i in range(2):
            child = pick([order[i], order[2 + i]], f)
            link = (
                link_ref[child]
                * below(one_ref[my_col * 2 + f], (b1, b2), 0)
                * below(two_ref[my_col * 4 + child], (b1, b2), 1)
            )
            both = (on * second_ref[my_row, my_col * 4 + child]).astype(F32)
            near = dot3(y1, halves(link), NN)
            out2[:, pl.ds(pl.multiple_of(child * b2, 128), b2)] = (near - y2[:, i * b2 : (i + 1) * b2]) * both


def finish_blocks(
    own, near, far, pivot1_ref, link_ref, pivot2_ref, parent_ref, one_ref, two_ref, out_diag, out_link, out_last, d_ref
):
    my_row, my_col = lax.axis_index("prow"), lax.axis_index("pcol")
    y, k = my_row % 2, my_col % 2
    b1, b2 = link_ref.shape[1:]
    order = family_order(parent_ref, my_col)
    for f, sums in ((1 - y, near[...]), (y, jnp.where(k == y, own[...], far[...]))):
        line = sums[b2 : b2 + 1]
        sums = sums[:b2]
        upper, lower = unfold(sums[:, 2 * b2 : 3 * b2], line[:, 2 * b2 : 3 * b2])
        d_ref[:b2, :b2] = upper
        d_ref[:b2, b2:] = sums[:, 5 * b2 : 6 * b2]
        d_ref[b2:, :b2] = sums[:, 5 * b2 : 6 * b2].T
        d_ref[b2:, b2:] = lower
        energy = unfold(sums[:, 6 * b2 :], line[:, 6 * b2 :])
        crosses = jnp.concatenate([sums[:, : 2 * b2], sums[:, 3 * b2 : 5 * b2]], axis=0)
        size = one_ref[my_col * 2 + f]
        diag = pivot1_ref[f] * below(size, (b1, b1), 0) * below(size, (b1, b1), 1) + d_ref[...]
        out_diag[f] = diag
        diag = halves(diag)
        for i in range(2):
            child = pick([order[i], order[2 + i]], f)
            width = two_ref[my_col * 4 + child]
            link = halves(link_ref[child] * below(size, (b1, b2), 0) * below(width, (b1, b2), 1))
            cross = crosses[:, i * b2 : (i + 1) * b2]
            down = cross - dot3(diag, link, NN)
            out_link[child] = down
            pivot = pivot2_ref[child] * below(width, (b2, b2), 0) * below(width, (b2, b2), 1)
            out_last[child] = pivot - dot3(link, halves(down), TN) - dot3(halves(cross), link, TN) + energy[i]


def call(body, outs, ins, scratch=(), scalars=0, name=None, room=8):
    specs = [VMEM] * (len(ins) - scalars) + [SMEM] * scalars
    return pl.pallas_call(
        body,
        out_shape=outs,
        in_specs=specs,
        out_specs=[VMEM] * len(outs),
        scratch_shapes=list(scratch),
        name=name,
        compiler_params=pltpu.CompilerParams(vmem_limit_bytes=room * 2**20),
        cost_estimate=FREE,
    )(*ins)


def array(*shape, dtype=F32):
    return jax.ShapeDtypeStruct(shape, dtype)


def solution(mesh):
    rows_of, cols_of = mesh.shape["prow"], mesh.shape["pcol"]
    depth, wide = rows_of // 2, cols_of // 2

    def pairs(move):
        out = []
        for z in range(depth):
            for y in range(2):
                for x in range(wide):
                    for k in range(2):
                        to = move(z, y, x, k)
                        if to is not None:
                            a, b, c, d = to
                            out.append(((z * 2 + y) * cols_of + x * 2 + k, (a * 2 + b) * cols_of + c * 2 + d))
        return out

    to_worker = pairs(lambda z, y, x, k: (z, y, x, 1 - k) if k == y else (z, 1 - y, x, k))
    to_home = pairs(lambda z, y, x, k: (z, 1 - y, x, k) if k == y else (z, y, x, 1 - k))
    across = pairs(lambda z, y, x, k: None if k == y else (z, 1 - y, x, 1 - k))
    other_y = pairs(lambda z, y, x, k: (z, 1 - y, x, k))
    other_core = pairs(lambda z, y, x, k: (z, y, x, 1 - k))
    up = pairs(lambda z, y, x, k: (z + 1, y, x, k) if z + 1 < depth else None)
    down = pairs(lambda z, y, x, k: (z - 1, y, x, k) if z > 0 else None)

    def send(value, perm):
        return lax.ppermute(value, AXES, perm)

    def on_device(
        anc_inverse,
        factor_one,
        pivot_one,
        factor_two,
        factor_link,
        pivot_two,
        pattern_one,
        pattern_two,
        parent_two,
        size_one,
        size_two,
    ):
        rows, tile = anc_inverse.shape
        total = tile * cols_of
        span = 2 * rows
        b1, b2 = pivot_one.shape[1], pivot_two.shape[1]
        z = lax.axis_index("prow") // 2
        block = array(b1, rows)
        scalars = [pattern_one, pattern_two, parent_two, size_one, size_two]

        def tie(*values):
            return lax.optimization_barrier(values)

        piece = array(b1 // CHUNKS, span)
        turns = [pairs(lambda z, y, x, k: (z, y, (x + s) % wide, k)) for s in range(1, wide)]
        tops = [send(anc_inverse, turn) for turn in turns]
        beside = send(anc_inverse, other_y)
        beside, *tops = tie(beside, *tops)
        kept1, give1 = call(pack_one, [block] * 2, [factor_one, pattern_one, size_one], scalars=2, name="pack_one")
        near1, far1 = send(give1, to_worker), send(kept1, across)
        factor_two, _ = tie(factor_two, give1)
        kept2, give2 = call(
            pack_two,
            [block] * 2,
            [factor_two, pattern_one, pattern_two, parent_two, size_two],
            scalars=4,
            name="pack_two",
        )
        near1, far1, kept2, give2 = tie(near1, far1, kept2, give2)
        (w1,) = call(join, [array(b1, span)], [kept1, near1, far1], name="join_one")
        near2, far2 = send(give2, to_worker), send(kept2, across)
        (w2,) = call(join, [array(b1, span)], [kept2, near2, far2], name="join_two")
        passed, _ = tie(beside, w1)
        middle = rows * 5 // 64 * 8
        tiles = [[anc_inverse, beside]]
        for turn, top in zip(turns, tops):
            tiles.append([top, send(passed[:middle], turn), send(top[middle:], other_y)])
        from_below, from_above = [send(w1, up)], [send(w1, down)]
        w2, from_below, from_above = tie(w2, from_below, from_above)
        panel = []
        for mine in tiles:
            panel += mine + [send(v, other_core) for v in mine]
        parts, high, low = call(
            functools.partial(partial_products, wide, [len(m) for m in tiles for _ in range(2)]),
            [array(b1, total), array(span, total, dtype=jnp.bfloat16), array(span, total, dtype=jnp.bfloat16)],
            [w2] + panel,
            name="partial_products",
            room=20,
        )

        def combined(s, c, from_below, from_above):
            whole = pl.BlockSpec(piece.shape, lambda i, at: (0, 0))
            taken = pl.BlockSpec(piece.shape, lambda i, at: (c if s == 2 else 0, 0))
            spec = pltpu.PrefetchScalarGridSpec(
                num_scalar_prefetch=1,
                grid=(1,),
                in_specs=[
                    taken,
                    taken,
                    pl.BlockSpec(piece.shape, lambda i, at: (c, jnp.clip(at[0] + 1 + depth - s, 0, depth - 1))),
                    pl.BlockSpec(piece.shape, lambda i, at: (c, jnp.clip(at[0] - 1 - depth + s, 0, depth - 1))),
                ],
                out_specs=[whole, whole],
            )

            def body(at_ref, *refs):
                combine(depth, s, *refs)

            return pl.pallas_call(
                body,
                grid_spec=spec,
                out_shape=[piece] * 2,
                name="combine",
                cost_estimate=FREE,
                compiler_params=pltpu.CompilerParams(vmem_limit_bytes=8 * 2**20),
            )(z[None], from_below, from_above, parts, parts)

        half = b1 // 2
        for s in range(1, depth):
            taken, chunks = from_below + from_above, len(from_below)
            blocks = range(CHUNKS)
            go = [combined(s + 1, c, from_below[c % chunks], from_above[c % chunks]) for c in blocks]
            from_below = [send(go[c][0], up) for c in blocks]
            from_above = [send(go[c][1], down) for c in blocks]
            if s == 1:
                (y1,) = call(own_product, [array(b1, span)], [high, low, w1], name="own_product", room=20)
            if s < depth - 1:
                (y1,) = call(
                    functools.partial(next_product, depth, s, chunks),
                    [array(b1, span)],
                    [high, low, y1] + taken,
                    name="next_product",
                    room=20,
                )
            if s == depth - 1:
                y1, mine, theirs = call(
                    functools.partial(gram_products, depth, s, chunks),
                    [array(b1, span)] + [array(half + 8, 3 * half)] * 2,
                    [high, low, y1] + taken + [w1, w2],
                    scratch=[pltpu.VMEM((b1, span), F32)],
                    name="gram_products",
                    room=20,
                )

        def swap(value, step):
            return send(value, pairs(lambda z, y, x, k: (z ^ step, y, x, k)))

        def deliver(same, give, other):
            return [same, send(give, to_home), send(other, across)]

        grams = mine + swap(theirs, 1)
        grams, from_below[0], from_above[0] = tie(grams, from_below[0], from_above[0])
        step = 2
        while 2 * step < depth:
            grams = grams + swap(grams, step)
            step *= 2
        arrived = swap(grams, step)

        def last_part():
            whole = pl.BlockSpec((b1, span), lambda i, at: (0, 0))
            part = pl.BlockSpec(piece.shape, lambda i, at: (0, 0))
            small = pl.BlockSpec((2 * b1, rows), lambda i, at: (0, 0))
            spec = pltpu.PrefetchScalarGridSpec(
                num_scalar_prefetch=1,
                grid=(1,),
                in_specs=[pl.BlockSpec((b1, span), lambda i, at: (0, at[0]))] + [part] * (2 * CHUNKS) + [whole, whole],
                out_specs=[small] * 3 + [pl.BlockSpec((b2 + 8, b2), lambda i, at: (0, 0))],
            )

            def body(at_ref, *refs):
                energy_products(CHUNKS, *refs)

            return pl.pallas_call(
                body,
                grid_spec=spec,
                out_shape=[array(2 * b1, rows)] * 3 + [array(b2 + 8, b2)],
                name="energy",
                cost_estimate=FREE,
                compiler_params=pltpu.CompilerParams(vmem_limit_bytes=12 * 2**20),
            )(z[None], parts, *from_below, *from_above, w2, y1)

        same, other, give, energy = last_part()
        home = deliver(same, give, other)
        step = 1
        while 2 * step < depth:
            energy = energy + swap(energy, step)
            step *= 2
        arrived, _ = tie(arrived, energy)
        grams = grams + arrived
        grams_too = swap(grams, 1)
        energies = [energy, swap(energy, step)]
        (sums,) = call(
            functools.partial(collect, depth), [array(half + 8, 7 * half)], [grams, grams_too] + energies, name="collect"
        )
        sums = deliver(sums, sums, sums)
        inverse_one, inverse_two = call(
            finish_rows,
            [array(rows, 2 * b1), array(rows, 4 * b2)],
            home + [factor_link] + scalars,
            scalars=5,
            name="finish_rows",
            room=16,
        )

        diagonal_one, inverse_link, diagonal_two = call(
            finish_blocks,
            [array(*pivot_one.shape), array(*factor_link.shape), array(*pivot_two.shape)],
            sums + [pivot_one, factor_link, pivot_two] + scalars[2:],
            scratch=[pltpu.VMEM((b1, b1), F32)],
            scalars=3,
            name="finish_blocks",
            room=16,
        )
        return inverse_one, diagonal_one, inverse_two, inverse_link, diagonal_two

    return jax.shard_map(
        on_device,
        mesh=mesh,
        in_specs=(
            P("prow", "pcol"),
            P("prow", "pcol"),
            P("pcol", None, None),
            P("prow", "pcol"),
            P("pcol", None, None),
            P("pcol", None, None),
            P(),
            P(),
            P(),
            P(),
            P(),
        ),
        out_specs=(
            P("prow", "pcol"),
            P("pcol", None, None),
            P("prow", "pcol"),
            P("pcol", None, None),
            P("pcol", None, None),
        ),
        check_vma=False,
    )
```
